256 devices in a mesh: resp: 64 (over x, y_lo, z), kvh: 4 (over y_hi, core).
Axes of the slice: x: 4, y: 4 (y_hi: 2, y_lo: 2; y = y_hi * 2 + y_lo), z: 8, core: 2. Of those that a mesh axis runs over, the one named last changes fastest.
Arguments:
- query: bfloat16 [16384, 5120], P('resp', 'kvh'), may hold values from -5 to 5
- response_keys: bfloat16 [16384, 1024], P('resp', 'kvh'), may hold values from -5 to 5
- response_values: bfloat16 [16384, 1024], P('resp', 'kvh'), may hold values from -5 to 5
- prompt_key: bfloat16 [2048, 1024], P(('resp', 'kvh')), may hold values from -5 to 5
- prompt_values: bfloat16 [2048, 1024], P(('resp', 'kvh')), may hold values from -5 to 5
- out_grad: bfloat16 [16384, 5120], P('resp', 'kvh'), may hold values from -5 to 5
- lengths: int32 [64, 2], P('resp'), may hold values from 1 to 192, 256 in all within a row
- advantage: float32 [64, 2], P('resp'), may hold values from -3 to 3
Outputs:
- grad_query: bfloat16 [16384, 5120], P('resp', 'kvh')
- grad_resp_key: bfloat16 [16384, 1024], P('resp', 'kvh')
- grad_resp_value: bfloat16 [16384, 1024], P('resp', 'kvh')
- grad_prompt_key: float32 [2048, 1024], P(('resp', 'kvh'))
- grad_prompt_value: float32 [2048, 1024], P(('resp', 'kvh'))
The draws below stay inside these ranges and needn't reach their ends.
Inputs may be any that keep to these rules, and one draw needn't show every extreme that they name: Each row of lengths sums to 256; its split into two lengths is drawn at random.
All inputs are finite; a program needn't handle non-finite values.
Results may differ from the reference program's by a relative error of at most 0.012.
Values may be sent and summed in bfloat16 or wider, within the bound.
No kernel may reach another device: no remote copies, remote signals or barrier semaphores. Data moves between devices by JAX's collectives and lax.ppermute only.
A program may use at most 128 MiB of HBM per device.

```python
import math
import jax
import jax.numpy as jnp
import numpy as np
from jax import lax

QUERY_HEADS = 40
KEY_VALUE_HEADS = 8
HEAD_SIZE = 128
TOK_DEV = 256
RESP_DEV = 2
PACKED_TOKENS = 16384
RESPONSES = 128
PROMPT_TOKENS = 2048
N_RESP = 64


def draw_query(key, part):
    key = jax.random.fold_in(key, 1)
    value_block = jnp.clip(jax.random.normal(key, (PACKED_TOKENS, QUERY_HEADS * HEAD_SIZE), jnp.float32), -4.5, 4.5)
    return value_block.astype(jnp.bfloat16)


def draw_prompt_key(key, part):
    key = jax.random.fold_in(key, 2)
    value_block = jnp.clip(jax.random.normal(key, (PROMPT_TOKENS, KEY_VALUE_HEADS * HEAD_SIZE), jnp.float32), -4.5, 4.5)
    return value_block.astype(jnp.bfloat16)


def steps_of(rng, dims, split, low, top_value):
    level, own = 1.0, jax.random.fold_in(rng, 6)
    for dim, parts in split:
        heights = jnp.exp(jax.random.uniform(jax.random.fold_in(own, dim), (parts,), jnp.float32, low / len(split), top_value / len(split)))
        level = level * jnp.repeat(heights, dims[dim] // parts).reshape([-1 if axis == dim else 1 for axis in range(len(dims))])
    return level


def split_up(number_of, total, most, skew):
    loads = [(1 << 20) // math.isqrt(grade ** skew) + 1 for grade in range(2, number_of + 1)]
    rest, holding = total - most - (number_of - 1), [1] * (number_of - 1)
    while rest > 0:
        free = [i for i in range(number_of - 1) if holding[i] < most]
        pool, remaining = sum([loads[i] for i in free]), rest
        for i in free:
            addition = min(most - holding[i], max(1, remaining * loads[i] // pool), rest)
            holding[i] = holding[i] + addition
            rest = rest - addition
    return np.array([most] + holding)


def uneven(key, amount, total, most, lean):
    if amount == 2:
        one = jax.random.randint(key, (), max(1, total - most), min(most, total - 1) + 1)
        return jnp.stack([one, total - one])
    sizes = jnp.asarray(split_up(amount, total, most, lean), jnp.int32)
    twos = (amount - 1) // 2
    source_of, sink = sizes[1:1 + 2 * twos:2], sizes[2:2 + 2 * twos:2]
    slack = jnp.minimum(source_of - 1, most - sink)
    passed = jax.random.randint(jax.random.fold_in(key, 1), (twos,), 0, 1 << 20) % (slack + 1)
    sizes = sizes.at[1:1 + 2 * twos:2].set(source_of - passed).at[2:2 + 2 * twos:2].set(sink + passed)
    return sizes[jax.random.permutation(jax.random.fold_in(key, 2), amount)]


def bell_draw(key, shape, width, bound, pieces=(), held_as=jnp.bfloat16):
    values = jax.random.normal(key, shape, jnp.float32) * width
    if len(pieces) > 0:
        values = steps_of(key, shape, pieces, -0.22, 0.18) * values
    return jnp.clip(values, min=-bound, max=bound).astype(held_as)


def setup_inputs(seed: int = 0) -> dict:
    arg_keys = jax.random.split(jax.random.key(seed), 9)
    query = draw_query(jax.random.fold_in(arg_keys[8], 71), 0)
    response_keys = bell_draw(arg_keys[1], (PACKED_TOKENS, KEY_VALUE_HEADS * HEAD_SIZE), 1.0, 5.0, ((0, 64), (1, 4)))
    response_values = bell_draw(arg_keys[2], (PACKED_TOKENS, KEY_VALUE_HEADS * HEAD_SIZE), 1.0, 5.0, ((0, 64), (1, 4)))
    prompt_key = draw_prompt_key(jax.random.fold_in(arg_keys[8], 71), 0)
    prompt_values = bell_draw(arg_keys[4], (PROMPT_TOKENS, KEY_VALUE_HEADS * HEAD_SIZE), 1.0, 5.0, ((0, 256),))
    out_grad = bell_draw(arg_keys[5], (PACKED_TOKENS, QUERY_HEADS * HEAD_SIZE), 1.0, 5.0, ((0, 64), (1, 4)))
    lengths = jax.vmap(lambda own: uneven(own, RESP_DEV, TOK_DEV, 3 * TOK_DEV // 4, 2))(jax.random.split(arg_keys[6], N_RESP)).reshape((N_RESP, RESP_DEV)).astype(jnp.int32)
    advantage = bell_draw(arg_keys[7], (N_RESP, RESP_DEV), 1.0, 3.0, ((0, 64),), jnp.float32)
    return {"query": query, "response_keys": response_keys, "response_values": response_values, "prompt_key": prompt_key, "prompt_values": prompt_values, "out_grad": out_grad, "lengths": lengths, "advantage": advantage}


def attend_block(query_row_block, gradient_rows, key_row_block, value_row_block, allowed):
    row_counts = query_row_block.shape[0]
    query_group = QUERY_HEADS // KEY_VALUE_HEADS
    factor = 1.0 / math.sqrt(HEAD_SIZE)
    query_block = query_row_block.reshape(row_counts, KEY_VALUE_HEADS, query_group, HEAD_SIZE).astype(jnp.float32)
    gradient_list = gradient_rows.reshape(row_counts, KEY_VALUE_HEADS, query_group, HEAD_SIZE).astype(jnp.float32)
    every_key = key_row_block.reshape(-1, KEY_VALUE_HEADS, HEAD_SIZE).astype(jnp.float32)
    every_value = value_row_block.reshape(-1, KEY_VALUE_HEADS, HEAD_SIZE).astype(jnp.float32)
    scores = jnp.einsum('bhgd,khd->hgbk', query_block, every_key) * factor
    scores = jnp.where(allowed[None, None], scores, -1e+30)
    row_peak = lax.optimization_barrier(jnp.max(scores, axis=-1, keepdims=True))
    expo = jnp.exp(scores - row_peak)
    softmax = expo / lax.optimization_barrier(jnp.sum(expo, axis=-1, keepdims=True))
    rounded_length = lax.optimization_barrier(softmax.astype(jnp.bfloat16)).astype(jnp.float32)
    attended = jnp.einsum('hgbk,khd->bhgd', rounded_length, every_value)
    row_delta = jnp.transpose(lax.optimization_barrier(jnp.sum(gradient_list * attended, axis=-1)), (1, 2, 0))
    prob_grad = jnp.einsum('bhgd,khd->hgbk', gradient_list, every_value)
    score_gradient = softmax * (prob_grad - row_delta[..., None]) * factor
    score_gradient = lax.optimization_barrier(score_gradient.astype(jnp.bfloat16)).astype(jnp.float32)
    query_grad = jnp.einsum('hgbk,khd->bhgd', score_gradient, every_key).reshape(row_counts, QUERY_HEADS * HEAD_SIZE)
    key_gradient = jnp.einsum('rlev,erlp->vrp', score_gradient, query_block).reshape(-1, KEY_VALUE_HEADS * HEAD_SIZE)
    value_gradient = jnp.einsum('rlev,erlp->vrp', rounded_length, gradient_list).reshape(-1, KEY_VALUE_HEADS * HEAD_SIZE)
    return (query_grad, key_gradient, value_gradient)

def reference(query, response_keys, response_values, prompt_key, prompt_values, out_grad, lengths, advantage):
    flat_lengths = lengths.reshape(-1)
    flat_adv = advantage.reshape(-1)
    positions = jnp.arange(PACKED_TOKENS, dtype=jnp.int32)
    resp_ends = jnp.cumsum(flat_lengths).astype(jnp.int32)
    segment = lax.optimization_barrier(jnp.sum((positions[:, None] >= resp_ends[None, :]).astype(jnp.int32), axis=1)).astype(jnp.int32)
    labels = jnp.arange(RESPONSES, dtype=jnp.int32)
    weight = lax.optimization_barrier(jnp.sum(jnp.where(segment[:, None] == labels[None, :], flat_adv[None, :], 0.0), axis=1))
    grad_out = (weight[:, None] * out_grad.astype(jnp.float32)).astype(jnp.bfloat16)
    key_columns = KEY_VALUE_HEADS * HEAD_SIZE
    prompt_len = prompt_key.shape[0]

    def step(running, index):
        begin_row = (index * TOK_DEV).astype(jnp.int32)
        query_row_block = lax.dynamic_slice_in_dim(query, begin_row, TOK_DEV, 0)
        gradient_rows = lax.dynamic_slice_in_dim(grad_out, begin_row, TOK_DEV, 0)
        near_key = lax.dynamic_slice_in_dim(response_keys, begin_row, TOK_DEV, 0)
        near_value = lax.dynamic_slice_in_dim(response_values, begin_row, TOK_DEV, 0)
        block_seg = lax.dynamic_slice_in_dim(segment, begin_row, TOK_DEV, 0)
        block_pos = lax.dynamic_slice_in_dim(positions, begin_row, TOK_DEV, 0)
        allowed_near = (block_seg[None, :] == block_seg[:, None]) & (block_pos[None, :] <= block_pos[:, None])
        allowed = jnp.concatenate([jnp.ones((TOK_DEV, prompt_len), bool), allowed_near], 1)
        key_row_block = jnp.concatenate([prompt_key, near_key], 0)
        value_row_block = jnp.concatenate([prompt_values, near_value], 0)
        query_grad, key_gradient, value_gradient = attend_block(query_row_block, gradient_rows, key_row_block, value_row_block, allowed)
        updated = (running[0] + key_gradient[:prompt_len], running[1] + value_gradient[:prompt_len])
        return (updated, (query_grad.astype(jnp.bfloat16), key_gradient[prompt_len:].astype(jnp.bfloat16), value_gradient[prompt_len:].astype(jnp.bfloat16)))
    start_state = (jnp.zeros((prompt_len, key_columns), jnp.float32), jnp.zeros((prompt_len, key_columns), jnp.float32))
    final, blocks = lax.scan(step, start_state, jnp.arange(PACKED_TOKENS // TOK_DEV, dtype=jnp.int32))
    grad_query = blocks[0].reshape(PACKED_TOKENS, QUERY_HEADS * HEAD_SIZE)
    grad_resp_key = blocks[1].reshape(PACKED_TOKENS, key_columns)
    grad_resp_value = blocks[2].reshape(PACKED_TOKENS, key_columns)
    return (grad_query, grad_resp_key, grad_resp_value, final[0], final[1])
```

```python
import functools
import math

import jax
import jax.numpy as jnp
from jax import lax
from jax.experimental import pallas as pl
from jax.experimental.pallas import tpu as pltpu
from jax.sharding import Mesh
from jax.sharding import PartitionSpec as P

QUERY_HEADS = 40
KEY_VALUE_HEADS = 8
HEAD = 128
GROUP = QUERY_HEADS // KEY_VALUE_HEADS
CHUNK = 256
LOG2E = 1.4426950408889634

NT = (((1,), (1,)), ((), ()))
NN = (((1,), (0,)), ((), ()))


def dot(a, b, dims):
    return lax.dot_general(a, b, dims, preferred_element_type=jnp.float32)


def attention_kernel(
    len_ref, adv_ref, q_ref, og_ref, nk_ref, nv_ref, kv_ref,
    gq_ref, gnk_ref, gnv_ref, gkv_ref,
    s_ref, dp_ref, acc_ref, kt_ref,
):
    g = pl.program_id(1)
    tokens = q_ref.shape[0]
    prompt = kv_ref.shape[0]
    chunks = prompt // CHUNK
    factor = 1.0 / math.sqrt(HEAD)
    responses = len_ref.shape[1]

    ends = []
    total = 0
    for r in range(responses):
        total = total + len_ref[0, r]
        ends.append(total)

    def segment(pos):
        seg = jnp.zeros(pos.shape, jnp.int32)
        for end in ends:
            seg = seg + (pos >= end).astype(jnp.int32)
        return seg

    tok = lax.broadcasted_iota(jnp.int32, (tokens, HEAD), 0)
    tok_seg = segment(tok)
    weight = jnp.zeros((tokens, HEAD), jnp.float32)
    for r in range(responses):
        weight = jnp.where(tok_seg == r, adv_ref[0, r], weight)

    q = q_ref[...]
    do = (weight * og_ref[...].astype(jnp.float32)).astype(jnp.bfloat16)

    @pl.when(g == 0)
    def _():
        acc_ref[...] = jnp.zeros_like(acc_ref)
        for c in range(chunks):
            kt_ref[:, c * CHUNK:(c + 1) * CHUNK] = (
                kv_ref[c * CHUNK:(c + 1) * CHUNK, :HEAD].astype(jnp.float32).T.astype(jnp.bfloat16)
            )
        kt_ref[:, prompt:] = nk_ref[...].astype(jnp.float32).T.astype(jnp.bfloat16)

    def rows(c):
        return slice(c * CHUNK, (c + 1) * CHUNK)

    def keys(c):
        return kv_ref[rows(c), :HEAD] if c < chunks else nk_ref[...]

    def values(c):
        return kv_ref[rows(c), HEAD:] if c < chunks else nv_ref[...]

    peak = jnp.full((1, tokens), -jnp.inf, jnp.float32)
    for c in range(chunks + 1):
        s = dot(keys(c), q, NT)
        if c == chunks:
            u = lax.broadcasted_iota(jnp.int32, (tokens, tokens), 0)
            t = lax.broadcasted_iota(jnp.int32, (tokens, tokens), 1)
            s = jnp.where((segment(u) == segment(t)) & (u <= t), s, -1e30)
        peak = jnp.maximum(peak, jnp.max(s, axis=0, keepdims=True))
        s_ref[rows(c), :] = s
        dp_ref[rows(c), :] = dot(values(c), do, NT)

    scale = factor * LOG2E
    shift = peak * scale
    row_sum = jnp.zeros((1, tokens), jnp.float32)
    weighted = jnp.zeros((1, tokens), jnp.float32)
    for c in range(chunks + 1):
        p = jnp.exp2(s_ref[rows(c), :] * scale - shift)
        s_ref[rows(c), :] = p
        row_sum = row_sum + jnp.sum(p, axis=0, keepdims=True)
        weighted = weighted + jnp.sum(p * dp_ref[rows(c), :], axis=0, keepdims=True)
    inverse = 1.0 / row_sum
    delta = weighted * inverse

    gq = jnp.zeros((HEAD, tokens), jnp.float32)
    for c in range(chunks + 1):
        p = s_ref[rows(c), :] * inverse
        ds = (p * (dp_ref[rows(c), :] - delta)).astype(jnp.bfloat16)
        acc_ref[rows(c), :HEAD] += dot(ds, q, NN)
        acc_ref[rows(c), HEAD:] += dot(p.astype(jnp.bfloat16), do, NN)
        gq = gq + dot(kt_ref[:, rows(c)], ds, NN)
    gq_ref[...] = (gq.T * factor).astype(jnp.bfloat16)

    @pl.when(g == GROUP - 1)
    def _():
        for c in range(chunks):
            gkv_ref[rows(c), :HEAD] = (acc_ref[rows(c), :HEAD] * factor).astype(jnp.bfloat16)
            gkv_ref[rows(c), HEAD:] = acc_ref[rows(c), HEAD:].astype(jnp.bfloat16)
        gnk_ref[...] = (acc_ref[prompt:, :HEAD] * factor).astype(jnp.bfloat16)
        gnv_ref[...] = acc_ref[prompt:, HEAD:].astype(jnp.bfloat16)


def attention(query, near_key, near_value, kv, out_grad, lengths, advantage):
    tokens = query.shape[0]
    prompt = kv.shape[0]
    heads = near_key.shape[1] // HEAD
    span = prompt + tokens
    smem = pl.BlockSpec(memory_space=pltpu.SMEM)
    by_query = pl.BlockSpec((tokens, HEAD), lambda h, g: (0, h * GROUP + g))
    by_head = pl.BlockSpec((tokens, HEAD), lambda h, g: (0, h))
    by_pair = pl.BlockSpec((prompt, 2 * HEAD), lambda h, g: (0, h))
    return pl.pallas_call(
        attention_kernel,
        grid=(heads, GROUP),
        in_specs=[smem, smem, by_query, by_query, by_head, by_head, by_pair],
        out_specs=[by_query, by_head, by_head, by_pair],
        out_shape=[
            jax.ShapeDtypeStruct(query.shape, jnp.bfloat16),
            jax.ShapeDtypeStruct(near_key.shape, jnp.bfloat16),
            jax.ShapeDtypeStruct(near_key.shape, jnp.bfloat16),
            jax.ShapeDtypeStruct(kv.shape, jnp.bfloat16),
        ],
        scratch_shapes=[
            pltpu.VMEM((span, tokens), jnp.float32),
            pltpu.VMEM((span, tokens), jnp.float32),
            pltpu.VMEM((span, 2 * HEAD), jnp.float32),
            pltpu.VMEM((HEAD, span), jnp.bfloat16),
        ],
        compiler_params=pltpu.CompilerParams(
            dimension_semantics=("arbitrary", "arbitrary"),
            vmem_limit_bytes=48 * 1024 * 1024,
        ),
        cost_estimate=pl.CostEstimate(
            flops=2 * 6 * heads * GROUP * tokens * span * HEAD,
            bytes_accessed=8 * 1024 * 1024,
            transcendentals=heads * GROUP * tokens * span,
        ),
        name="attention",
    )(lengths, advantage, query, out_grad, near_key, near_value, kv)


NEAR = ("z", "kvh")
FAR = ("x", "y")


def exchange(a, axes):
    return lax.all_to_all(a, axes, split_axis=0, concat_axis=0, tiled=True)


def on_device(
    shape, query, response_keys, response_values, prompt_key, prompt_values, out_grad, lengths,
    advantage
):
    x, y, z, kvh = shape
    own = prompt_key.shape[0]
    heads = response_keys.shape[1] // HEAD
    cols = 2 * heads * HEAD
    pairs = jnp.stack(
        [
            prompt_key.reshape(own, kvh, heads, HEAD),
            prompt_values.reshape(own, kvh, heads, HEAD),
        ],
        axis=3,
    ).reshape(own, kvh, cols)
    pairs = jnp.transpose(pairs, (1, 0, 2))
    sent = jnp.broadcast_to(pairs[None], (z, kvh, own, cols)).reshape(z * kvh * own, cols)
    block = exchange(sent, NEAR)
    rows = block.shape[0]
    kv = exchange(jnp.broadcast_to(block[None], (x * y, rows, cols)).reshape(x * y * rows, cols), FAR)

    grad_query, grad_resp_key, grad_resp_value, grad_kv = attention(
        query, response_keys, response_values, kv, out_grad, lengths, advantage
    )

    part = exchange(grad_kv, FAR).reshape(x * y, rows, cols)
    part = jnp.sum(part.astype(jnp.float32), axis=0).astype(jnp.bfloat16)
    part = exchange(part, NEAR).reshape(z, kvh, own, cols)
    grads = jnp.sum(part.astype(jnp.float32), axis=0).reshape(kvh, own, heads, 2, HEAD)
    grads = jnp.transpose(grads, (3, 1, 0, 2, 4)).reshape(2, own, kvh * heads * HEAD)
    return (grad_query, grad_resp_key, grad_resp_value, grads[0], grads[1])


def solution(mesh):
    x, y, z, kvh = 4, 2, 8, 4
    fine = Mesh(mesh.devices.reshape(x, y, z, kvh), ("x", "y", "z", "kvh"))
    resp = ("x", "y", "z")
    every = ("x", "y", "z", "kvh")
    return jax.shard_map(
        functools.partial(on_device, (x, y, z, kvh)),
        mesh=fine,
        in_specs=(
            P(resp, "kvh"),
            P(resp, "kvh"),
            P(resp, "kvh"),
            P(every, None),
            P(every, None),
            P(resp, "kvh"),
            P(resp, None),
            P(resp, None),
        ),
        out_specs=(
            P(resp, "kvh"),
            P(resp, "kvh"),
            P(resp, "kvh"),
            P(every, None),
            P(every, None),
        ),
        check_vma=False,
    )
```

```python
import functools
import math

import jax
import jax.numpy as jnp
from jax import lax
from jax.experimental import pallas as pl
from jax.experimental.pallas import tpu as pltpu
from jax.sharding import Mesh
from jax.sharding import PartitionSpec as P

QUERY_HEADS = 40
KEY_VALUE_HEADS = 8
HEAD = 128
GROUP = QUERY_HEADS // KEY_VALUE_HEADS
CHUNK = 256
LOG2E = 1.4426950408889634

NT = (((1,), (1,)), ((), ()))
NN = (((1,), (0,)), ((), ()))


def dot(a, b, dims):
    return lax.dot_general(a, b, dims, preferred_element_type=jnp.float32)


def attention_kernel(
    len_ref, adv_ref, q_ref, og_ref, nk_ref, nv_ref, kv_ref, *rest
):
    gq_ref, gnk_ref, gnv_ref, gkv_ref, s_ref, dp_ref, acc_ref, kt_ref = rest[-8:]
    g = pl.program_id(0)
    tokens = q_ref.shape[0]
    prompt = kv_ref.shape[0]
    chunks = prompt // CHUNK
    factor = 1.0 / math.sqrt(HEAD)
    responses = len_ref.shape[1]

    ends = []
    total = 0
    for r in range(responses):
        total = total + len_ref[0, r]
        ends.append(total)

    def segment(pos):
        seg = jnp.zeros(pos.shape, jnp.int32)
        for end in ends:
            seg = seg + (pos >= end).astype(jnp.int32)
        return seg

    tok = lax.broadcasted_iota(jnp.int32, (tokens, HEAD), 0)
    tok_seg = segment(tok)
    weight = jnp.zeros((tokens, HEAD), jnp.float32)
    for r in range(responses):
        weight = jnp.where(tok_seg == r, adv_ref[0, r], weight)

    q = q_ref[...]
    do = (weight * og_ref[...].astype(jnp.float32)).astype(jnp.bfloat16)

    @pl.when(g == 0)
    def _():
        acc_ref[...] = jnp.zeros_like(acc_ref)
        for c in range(chunks):
            kt_ref[:, c * CHUNK:(c + 1) * CHUNK] = (
                kv_ref[c * CHUNK:(c + 1) * CHUNK, :HEAD].astype(jnp.float32).T.astype(jnp.bfloat16)
            )
        kt_ref[:, prompt:] = nk_ref[...].astype(jnp.float32).T.astype(jnp.bfloat16)

    def rows(c):
        return slice(c * CHUNK, (c + 1) * CHUNK)

    def keys(c):
        return kv_ref[rows(c), :HEAD] if c < chunks else nk_ref[...]

    def values(c):
        return kv_ref[rows(c), HEAD:] if c < chunks else nv_ref[...]

    peak = jnp.full((1, tokens), -jnp.inf, jnp.float32)
    for c in range(chunks + 1):
        s = dot(keys(c), q, NT)
        if c == chunks:
            u = lax.broadcasted_iota(jnp.int32, (tokens, tokens), 0)
            t = lax.broadcasted_iota(jnp.int32, (tokens, tokens), 1)
            s = jnp.where((segment(u) == segment(t)) & (u <= t), s, -1e30)
        peak = jnp.maximum(peak, jnp.max(s, axis=0, keepdims=True))
        s_ref[rows(c), :] = s
        dp_ref[rows(c), :] = dot(values(c), do, NT)

    scale = factor * LOG2E
    shift = peak * scale
    row_sum = jnp.zeros((1, tokens), jnp.float32)
    weighted = jnp.zeros((1, tokens), jnp.float32)
    for c in range(chunks + 1):
        p = jnp.exp2(s_ref[rows(c), :] * scale - shift)
        s_ref[rows(c), :] = p
        row_sum = row_sum + jnp.sum(p, axis=0, keepdims=True)
        weighted = weighted + jnp.sum(p * dp_ref[rows(c), :], axis=0, keepdims=True)
    inverse = 1.0 / row_sum
    delta = weighted * inverse

    gq = jnp.zeros((HEAD, tokens), jnp.float32)
    for c in range(chunks + 1):
        p = s_ref[rows(c), :] * inverse
        ds = (p * (dp_ref[rows(c), :] - delta)).astype(jnp.bfloat16)
        acc_ref[rows(c), :HEAD] += dot(ds, q, NN)
        acc_ref[rows(c), HEAD:] += dot(p.astype(jnp.bfloat16), do, NN)
        gq = gq + dot(kt_ref[:, rows(c)], ds, NN)
    gq_ref[...] = (gq.T * factor).astype(jnp.bfloat16)

    @pl.when(g == GROUP - 1)
    def _():
        for c in range(chunks):
            gkv_ref[rows(c), :HEAD] = (acc_ref[rows(c), :HEAD] * factor).astype(jnp.bfloat16)
            gkv_ref[rows(c), HEAD:] = acc_ref[rows(c), HEAD:].astype(jnp.bfloat16)
        gnk_ref[...] = (acc_ref[prompt:, :HEAD] * factor).astype(jnp.bfloat16)
        gnv_ref[...] = acc_ref[prompt:, HEAD:].astype(jnp.bfloat16)


def attention(head, query, near_key, near_value, kv, out_grad, lengths, advantage, before):
    tokens = query.shape[0]
    prompt = kv.shape[0]
    span = prompt + tokens
    smem = pl.BlockSpec(memory_space=pltpu.SMEM)
    by_query = pl.BlockSpec((tokens, HEAD), lambda g: (0, head * GROUP + g))
    by_head = pl.BlockSpec((tokens, HEAD), lambda g: (0, head))
    whole = pl.BlockSpec((prompt, 2 * HEAD), lambda g: (0, 0))
    return pl.pallas_call(
        attention_kernel,
        grid=(GROUP,),
        in_specs=[smem, smem, by_query, by_query, by_head, by_head, whole]
        + [pl.BlockSpec(memory_space=pl.ANY)] * len(before),
        out_specs=[by_query, by_head, by_head, whole],
        out_shape=[
            jax.ShapeDtypeStruct(query.shape, jnp.bfloat16),
            jax.ShapeDtypeStruct(near_key.shape, jnp.bfloat16),
            jax.ShapeDtypeStruct(near_key.shape, jnp.bfloat16),
            jax.ShapeDtypeStruct(kv.shape, jnp.bfloat16),
        ],
        input_output_aliases={7 + i: i for i in range(len(before))},
        scratch_shapes=[
            pltpu.VMEM((span, tokens), jnp.float32),
            pltpu.VMEM((span, tokens), jnp.float32),
            pltpu.VMEM((span, 2 * HEAD), jnp.float32),
            pltpu.VMEM((HEAD, span), jnp.bfloat16),
        ],
        compiler_params=pltpu.CompilerParams(
            dimension_semantics=("arbitrary",),
            vmem_limit_bytes=40 * 1024 * 1024,
        ),
        cost_estimate=pl.CostEstimate(
            flops=2 * 6 * GROUP * tokens * span * HEAD,
            bytes_accessed=4 * 1024 * 1024,
            transcendentals=GROUP * tokens * span,
        ),
        name="attention",
    )(lengths, advantage, query, out_grad, near_key, near_value, kv, *before)


NEAR = ("zh", "kvh")
FAR = ("x", "y", "zl")


def exchange(a, axes):
    return lax.all_to_all(a, axes, split_axis=0, concat_axis=0, tiled=True)


def on_device(
    shape, query, response_keys, response_values, prompt_key, prompt_values, out_grad, lengths,
    advantage
):
    x, y, zh, zl, kvh = shape
    far = x * y * zl
    own = prompt_key.shape[0]
    heads = response_keys.shape[1] // HEAD
    cols = 2 * heads * HEAD
    pairs = jnp.stack(
        [
            prompt_key.reshape(own, kvh, heads, HEAD),
            prompt_values.reshape(own, kvh, heads, HEAD),
        ],
        axis=3,
    ).reshape(own, kvh, cols)
    pairs = jnp.transpose(pairs, (1, 0, 2))
    sent = jnp.broadcast_to(pairs[None], (zh, kvh, own, cols)).reshape(zh * kvh * own, cols)
    block = exchange(sent, NEAR)
    rows = block.shape[0]
    wide = 2 * HEAD

    def spread(head):
        part = block[:, head * wide:(head + 1) * wide]
        return exchange(jnp.broadcast_to(part[None], (far, rows, wide)).reshape(far * rows, wide), FAR)

    before = ()
    sums = []
    for head in range(heads):
        *before, grad_kv = attention(
            head, query, response_keys, response_values, spread(head), out_grad, lengths, advantage,
            before
        )
        part = exchange(grad_kv, FAR).reshape(far, rows, wide)
        sums.append(jnp.sum(part.astype(jnp.float32), axis=0).astype(jnp.bfloat16))
    part = exchange(jnp.concatenate(sums, axis=1), NEAR).reshape(zh, kvh, own, cols)
    grads = jnp.sum(part.astype(jnp.float32), axis=0).reshape(kvh, own, heads, 2, HEAD)
    grads = jnp.transpose(grads, (3, 1, 0, 2, 4)).reshape(2, own, kvh * heads * HEAD)
    return (*before, grads[0], grads[1])


def solution(mesh):
    shape = (4, 2, 4, 2, 4)
    names = ("x", "y", "zh", "zl", "kvh")
    fine = Mesh(mesh.devices.reshape(shape), names)
    resp = names[:4]
    return jax.shard_map(
        functools.partial(on_device, shape),
        mesh=fine,
        in_specs=(
            P(resp, "kvh"),
            P(resp, "kvh"),
            P(resp, "kvh"),
            P(names, None),
            P(names, None),
            P(resp, "kvh"),
            P(resp, None),
            P(resp, None),
        ),
        out_specs=(
            P(resp, "kvh"),
            P(resp, "kvh"),
            P(resp, "kvh"),
            P(names, None),
            P(names, None),
        ),
        check_vma=False,
    )
```

```python
import functools
import math

import jax
import jax.numpy as jnp
from jax import lax
from jax.experimental import pallas as pl
from jax.experimental.pallas import tpu as pltpu
from jax.sharding import Mesh
from jax.sharding import PartitionSpec as P

QUERY_HEADS = 40
KEY_VALUE_HEADS = 8
HEAD = 128
GROUP = QUERY_HEADS // KEY_VALUE_HEADS
CHUNK = 1024
FOLD = 16
VMEM_MIB = 38
TIE = True
HALF = (GROUP + 1) * HEAD
Q_COLS = slice(0, GROUP * HEAD)
K_COLS = slice(GROUP * HEAD, HALF)
O_COLS = slice(HALF, HALF + GROUP * HEAD)
V_COLS = slice(HALF + GROUP * HEAD, 2 * HALF)
GK_COLS = slice(GROUP * HEAD, (GROUP + 1) * HEAD)
GV_COLS = slice((GROUP + 1) * HEAD, (GROUP + 2) * HEAD)
LOG2E = 1.4426950408889634

NN = (((1,), (0,)), ((), ()))


def dot(a, b, dims):
    return lax.dot_general(a, b, dims, preferred_element_type=jnp.float32)


def attention_kernel(
    len_ref, adv_ref, got_ref, q_hbm, og_hbm, nk_hbm, nv_hbm, got_a_hbm, got_b_hbm, kv_hbm,
    gq_hbm, gnk_hbm, gnv_hbm, back_hbm, gkv_hbm,
    tok_ref, kv_ref, grad_ref, gkv_ref, sum_kv_ref,
    p_ref, d_ref, kt_ref, qt_ref, dot_t_ref, gqt_ref,
    peak_ref, sum_ref, dot_ref, in_sem, kv_sem, out_sem,
):
    tokens = tok_ref.shape[1]
    prompt = kv_ref.shape[0]
    chunks = prompt // CHUNK
    factor = 1.0 / math.sqrt(HEAD)
    scale = factor * LOG2E

    mine = lax.axis_index("zl")
    query_cols = pl.ds(pl.multiple_of(mine * (GROUP * HEAD), HEAD), GROUP * HEAD)
    own_cols = pl.ds(pl.multiple_of(mine * HEAD, HEAD), HEAD)
    own_loads = [
        pltpu.make_async_copy(q_hbm.at[:, query_cols], tok_ref.at[0, :, Q_COLS], in_sem.at[0]),
        pltpu.make_async_copy(og_hbm.at[:, query_cols], tok_ref.at[0, :, O_COLS], in_sem.at[1]),
        pltpu.make_async_copy(nk_hbm.at[:, own_cols], tok_ref.at[0, :, K_COLS], in_sem.at[2]),
        pltpu.make_async_copy(nv_hbm.at[:, own_cols], tok_ref.at[0, :, V_COLS], in_sem.at[3]),
    ]
    got_loads = [
        pltpu.make_async_copy(got_a_hbm, tok_ref.at[1, :, pl.ds(0, HALF)], in_sem.at[4]),
        pltpu.make_async_copy(got_b_hbm, tok_ref.at[1, :, pl.ds(HALF, HALF)], in_sem.at[5]),
    ]
    for copy in own_loads:
        copy.start()
    kv_loads = []
    for c in range(chunks):
        at = pl.ds(c * CHUNK, CHUNK)
        kv_loads.append(pltpu.make_async_copy(kv_hbm.at[at], kv_ref.at[at], kv_sem.at[c]))
        kv_loads[-1].start()
    for copy in got_loads:
        copy.start()

    responses = len_ref.shape[1]

    def segment(pos, ends):
        seg = jnp.zeros(pos.shape, jnp.int32)
        for end in ends:
            seg = seg + (pos >= end).astype(jnp.int32)
        return seg

    def head_cols(g, first=0):
        return slice(first + g * HEAD, first + (g + 1) * HEAD)

    def tok_cols(g):
        return slice(g * tokens, (g + 1) * tokens)

    def turn(a):
        return a.astype(jnp.float32).T.astype(jnp.bfloat16)

    def forward(keys, values, row, mask):
        size = keys.shape[0]
        groups = size // (8 * FOLD)
        for g in range(GROUP):
            s = dot(keys, qt_ref[:, tok_cols(g)], NN)
            if mask is not None:
                s = jnp.where(mask, s, -1e30)
            d = dot(values, dot_t_ref[:, tok_cols(g)], NN)
            s = s.reshape(groups, FOLD, 8, tokens)
            d_ref[row:row + size, tok_cols(g)] = d
            d = d.reshape(groups, FOLD, 8, tokens)
            for i in range(groups):
                slot = row // FOLD + 8 * i
                key = row + 8 * FOLD * i
                peak = jnp.max(s[i], axis=0)
                e = jnp.exp2((s[i] - peak[None]) * scale)
                p_ref[key:key + 8 * FOLD, tok_cols(g)] = e.reshape(8 * FOLD, tokens)
                peak_ref[slot:slot + 8, tok_cols(g)] = peak
                sum_ref[slot:slot + 8, tok_cols(g)] = jnp.sum(e, axis=0)
                dot_ref[slot:slot + 8, tok_cols(g)] = jnp.sum(e * d[i], axis=0)

    def backward(part, row, size, deltas):
        groups = size // (8 * FOLD)
        slot = row // FOLD
        key_sum = jnp.zeros((size, HEAD), jnp.float32)
        value_sum = jnp.zeros((size, HEAD), jnp.float32)
        for g in range(GROUP):
            p = p_ref[row:row + size, tok_cols(g)].reshape(groups, FOLD, 8, tokens)
            d = d_ref[row:row + size, tok_cols(g)].reshape(groups, FOLD, 8, tokens)
            share = peak_ref[slot:slot + 8 * groups, tok_cols(g)].reshape(groups, 1, 8, tokens)
            p = p * share
            ds = p * (d - deltas[g][None, None])
            p = p.reshape(size, tokens).astype(jnp.bfloat16)
            ds = ds.reshape(size, tokens).astype(jnp.bfloat16)
            key_sum = key_sum + dot(ds, tok_ref[part, :, head_cols(g)], NN)
            value_sum = value_sum + dot(p, tok_ref[part, :, head_cols(g, HALF)], NN)
            query_sum = dot(kt_ref[:, row:row + size], ds, NN)
            if row == 0:
                gqt_ref[:, tok_cols(g)] = query_sum
            else:
                gqt_ref[:, tok_cols(g)] += query_sum
        return key_sum * factor, value_sum

    stores = []

    def store(source, target):
        stores.append(pltpu.make_async_copy(source, target, out_sem.at[len(stores)]))
        stores[-1].start()

    parts = tok_ref.shape[0]
    for part in range(parts):
        if part == 0:
            lengths = [len_ref[0, r] for r in range(responses)]
            advantages = [adv_ref[0, r] for r in range(responses)]
        else:
            lengths = [got_ref[0, r].astype(jnp.int32) for r in range(responses)]
            advantages = [got_ref[0, responses + r] for r in range(responses)]
        ends = [sum(lengths[:r + 1]) for r in range(responses)]
        for copy in own_loads if part == 0 else got_loads:
            copy.wait()
        tok_seg = segment(lax.broadcasted_iota(jnp.int32, (tokens, HEAD), 0), ends)
        weight = jnp.zeros((tokens, HEAD), jnp.float32)
        for r in range(responses):
            weight = jnp.where(tok_seg == r, advantages[r], weight)
        for g in range(GROUP):
            cols = head_cols(g, HALF)
            do = weight * tok_ref[part, :, cols].astype(jnp.float32)
            tok_ref[part, :, cols] = do.astype(jnp.bfloat16)
        for g in range(GROUP):
            qt_ref[:, tok_cols(g)] = turn(tok_ref[part, :, head_cols(g)])
            dot_t_ref[:, tok_cols(g)] = turn(tok_ref[part, :, head_cols(g, HALF)])

        u = lax.broadcasted_iota(jnp.int32, (tokens, tokens), 0)
        t = lax.broadcasted_iota(jnp.int32, (tokens, tokens), 1)
        near = (segment(u, ends) == segment(t, ends)) & (u <= t)
        near_keys = tok_ref[part, :, K_COLS]
        kt_ref[:, prompt:] = turn(near_keys)
        forward(near_keys, tok_ref[part, :, V_COLS], prompt, near)
        for c in range(chunks):
            at = slice(c * CHUNK, (c + 1) * CHUNK)
            if part == 0:
                kv_loads[c].wait()
                kt_ref[:, at] = turn(kv_ref[at, :HEAD])
            forward(kv_ref[at, :HEAD], kv_ref[at, HEAD:], c * CHUNK, None)

        deltas = []
        for g in range(GROUP):
            peak = peak_ref[:, tok_cols(g)]
            top = jnp.max(peak, axis=0, keepdims=True)
            share = jnp.exp2((peak - top) * scale)
            row_sum = jnp.sum(share * sum_ref[:, tok_cols(g)], axis=0, keepdims=True)
            weighted = jnp.sum(share * dot_ref[:, tok_cols(g)], axis=0, keepdims=True)
            inverse = 1.0 / row_sum
            peak_ref[:, tok_cols(g)] = share * inverse
            deltas.append(jnp.broadcast_to(weighted * inverse, (8, tokens)))

        for c in range(chunks):
            at = slice(c * CHUNK, (c + 1) * CHUNK)
            key_grad, value_grad = backward(part, c * CHUNK, CHUNK, deltas)
            if part == 0:
                sum_kv_ref[at, :HEAD], sum_kv_ref[at, HEAD:] = key_grad, value_grad
            if part == parts - 1:
                gkv_ref[at, :HEAD] = (sum_kv_ref[at, :HEAD] + key_grad).astype(jnp.bfloat16)
                gkv_ref[at, HEAD:] = (sum_kv_ref[at, HEAD:] + value_grad).astype(jnp.bfloat16)
                store(gkv_ref.at[pl.ds(c * CHUNK, CHUNK)], gkv_hbm.at[pl.ds(c * CHUNK, CHUNK)])
        key_grad, value_grad = backward(part, prompt, tokens, deltas)
        grad_ref[part, :, GK_COLS] = key_grad.astype(jnp.bfloat16)
        grad_ref[part, :, GV_COLS] = value_grad.astype(jnp.bfloat16)
        for g in range(GROUP):
            grad_ref[part, :, head_cols(g)] = (gqt_ref[:, tok_cols(g)].T * factor).astype(jnp.bfloat16)
        if part == 0:
            store(grad_ref.at[0, :, Q_COLS], gq_hbm.at[:, query_cols])
            store(grad_ref.at[0, :, GK_COLS], gnk_hbm.at[:, own_cols])
            store(grad_ref.at[0, :, GV_COLS], gnv_hbm.at[:, own_cols])
        else:
            store(grad_ref.at[1], back_hbm)
    for copy in stores:
        copy.wait()


def attention(query, near_key, near_value, got_a, got_b, got, kv, out_grad, lengths, advantage):
    tokens = query.shape[0]
    prompt = kv.shape[0]
    span = prompt + tokens
    wide = GROUP * tokens
    back = (GROUP + 2) * HEAD
    smem = pl.BlockSpec(memory_space=pltpu.SMEM)
    here = pl.BlockSpec(memory_space=pl.ANY)
    bf16, f32 = jnp.bfloat16, jnp.float32
    return pl.pallas_call(
        attention_kernel,
        in_specs=[smem] * 3 + [here] * 7,
        out_specs=[here] * 5,
        out_shape=[
            jax.ShapeDtypeStruct(query.shape, bf16),
            jax.ShapeDtypeStruct(near_key.shape, bf16),
            jax.ShapeDtypeStruct(near_key.shape, bf16),
            jax.ShapeDtypeStruct((tokens, back), bf16),
            jax.ShapeDtypeStruct(kv.shape, bf16),
        ],
        scratch_shapes=[
            pltpu.VMEM((2, tokens, 2 * HALF), bf16),
            pltpu.VMEM((prompt, 2 * HEAD), bf16),
            pltpu.VMEM((2, tokens, back), bf16),
            pltpu.VMEM((prompt, 2 * HEAD), bf16),
            pltpu.VMEM((prompt, 2 * HEAD), f32),
            pltpu.VMEM((span, wide), f32),
            pltpu.VMEM((span, wide), f32),
            pltpu.VMEM((HEAD, span), bf16),
            pltpu.VMEM((HEAD, wide), bf16),
            pltpu.VMEM((HEAD, wide), bf16),
            pltpu.VMEM((HEAD, wide), f32),
            pltpu.VMEM((span // FOLD, wide), f32),
            pltpu.VMEM((span // FOLD, wide), f32),
            pltpu.VMEM((span // FOLD, wide), f32),
            pltpu.SemaphoreType.DMA((6,)),
            pltpu.SemaphoreType.DMA((prompt // CHUNK,)),
            pltpu.SemaphoreType.DMA((prompt // CHUNK + 4,)),
        ],
        compiler_params=pltpu.CompilerParams(vmem_limit_bytes=VMEM_MIB * 1024 * 1024),
        cost_estimate=pl.CostEstimate(
            flops=2 * 6 * 2 * GROUP * tokens * span * HEAD,
            bytes_accessed=8 * 1024 * 1024,
            transcendentals=2 * GROUP * tokens * span,
        ),
        name="attention",
    )(lengths, advantage, got, query, out_grad, near_key, near_value, got_a, got_b, kv)


NEAR = ("zh", "zl", "kvh")
FAR = ("x", "y")
SWAP = [(0, 1), (1, 0)]


def exchange(a, axes):
    return lax.all_to_all(a, axes, split_axis=0, concat_axis=0, tiled=True)


def pack_kernel(
    copies, len_ref, adv_ref, q_hbm, og_hbm, nk_hbm, nv_hbm, key_ref, value_ref,
    send_a_ref, send_b_ref, send_ref, first_ref, sem,
):
    other = 1 - lax.axis_index("zl")
    query_cols = pl.ds(pl.multiple_of(other * (GROUP * HEAD), HEAD), GROUP * HEAD)
    key_cols = pl.ds(pl.multiple_of(other * HEAD, HEAD), HEAD)
    moves = []
    for i, (source, cols, target, at) in enumerate([
        (q_hbm, query_cols, send_a_ref, pl.ds(0, GROUP * HEAD)),
        (nk_hbm, key_cols, send_a_ref, pl.ds(GROUP * HEAD, HEAD)),
        (og_hbm, query_cols, send_b_ref, pl.ds(0, GROUP * HEAD)),
        (nv_hbm, key_cols, send_b_ref, pl.ds(GROUP * HEAD, HEAD)),
    ]):
        moves.append(pltpu.make_async_copy(source.at[:, cols], target.at[:, at], sem.at[i]))
        moves[-1].start()
    responses = len_ref.shape[1]
    for r in range(responses):
        send_ref[0, r] = len_ref[0, r].astype(jnp.float32)
        send_ref[0, responses + r] = adv_ref[0, r]
    zl = 2
    kvh = KEY_VALUE_HEADS // zl
    rows = []
    for half in range(zl):
        for owner in range(kvh):
            cols = slice((owner * zl + half) * HEAD, (owner * zl + half + 1) * HEAD)
            rows.append(jnp.concatenate(
                [key_ref[:, cols].astype(jnp.float32), value_ref[:, cols].astype(jnp.float32)], axis=1
            ))
    rows = jnp.concatenate(rows, axis=0)
    count = rows.shape[0]
    rows = rows.astype(jnp.bfloat16)
    for c in range(copies):
        first_ref[c * count:(c + 1) * count, :] = rows
    for copy in moves:
        copy.wait()


def pack(copies, lengths, advantage, query, out_grad, near_key, near_value, key, value):
    tokens = query.shape[0]
    responses = lengths.shape[1]
    own = key.shape[0]
    smem = pl.BlockSpec(memory_space=pltpu.SMEM)
    vmem = pl.BlockSpec(memory_space=pltpu.VMEM)
    here = pl.BlockSpec(memory_space=pl.ANY)
    return pl.pallas_call(
        functools.partial(pack_kernel, copies),
        in_specs=[smem, smem] + [here] * 4 + [vmem] * 2,
        out_specs=[vmem, vmem, smem, vmem],
        out_shape=[
            jax.ShapeDtypeStruct((tokens, HALF), jnp.bfloat16),
            jax.ShapeDtypeStruct((tokens, HALF), jnp.bfloat16),
            jax.ShapeDtypeStruct((1, 2 * responses), jnp.float32),
            jax.ShapeDtypeStruct((copies * KEY_VALUE_HEADS * own, 2 * HEAD), jnp.bfloat16),
        ],
        scratch_shapes=[pltpu.SemaphoreType.DMA((4,))],
        name="pack",
    )(lengths, advantage, query, out_grad, near_key, near_value, key, value)


def finish(copies, part):
    rows = jnp.sum(part.astype(jnp.float32).reshape(copies, -1, 2 * HEAD), axis=0)
    zl = 2
    kvh = KEY_VALUE_HEADS // zl
    own = rows.shape[0] // KEY_VALUE_HEADS
    blocks = [
        rows[(half * kvh + owner) * own:(half * kvh + owner + 1) * own]
        for owner in range(kvh) for half in range(zl)
    ]
    return (
        jnp.concatenate([block[:, :HEAD] for block in blocks], axis=1),
        jnp.concatenate([block[:, HEAD:] for block in blocks], axis=1),
    )


def on_device(
    shape, query, response_keys, response_values, prompt_key, prompt_values, out_grad, lengths,
    advantage
):
    x, y, zh, zl, kvh = shape
    send_a, send_b, send, first = pack(
        zh, lengths, advantage, query, out_grad, response_keys, response_values, prompt_key,
        prompt_values
    )
    got_a = lax.ppermute(send_a, "zl", SWAP)
    got_b = lax.ppermute(send_b, "zl", SWAP)
    got = lax.ppermute(send, "zl", SWAP)

    block = exchange(first, NEAR)
    if TIE:
        block, got_a = lax.optimization_barrier((block, got_a))
    kv = exchange(jnp.broadcast_to(block[None], (x * y, *block.shape)).reshape(-1, 2 * HEAD), FAR)

    grad_query, grad_resp_key, grad_resp_value, back, grad_kv = attention(
        query, response_keys, response_values, got_a, got_b, got, kv, out_grad, lengths, advantage
    )

    back = lax.ppermute(back, "zl", SWAP)
    part = exchange(grad_kv, FAR).reshape(x * y, *block.shape)
    part = jnp.sum(part.astype(jnp.float32), axis=0).astype(jnp.bfloat16)
    grad_prompt_key, grad_prompt_value = finish(zh, exchange(part, NEAR))

    other = 1 - lax.axis_index("zl")
    grad_query = lax.dynamic_update_slice(grad_query, back[:, Q_COLS], (0, other * GROUP * HEAD))
    grad_resp_key = lax.dynamic_update_slice(grad_resp_key, back[:, GK_COLS], (0, other * HEAD))
    grad_resp_value = lax.dynamic_update_slice(grad_resp_value, back[:, GV_COLS], (0, other * HEAD))
    return (grad_query, grad_resp_key, grad_resp_value, grad_prompt_key, grad_prompt_value)


def solution(mesh):
    shape = (4, 2, 4, 2, 4)
    names = ("x", "y", "zh", "zl", "kvh")
    fine = Mesh(mesh.devices.reshape(shape), names)
    resp = names[:4]
    return jax.shard_map(
        functools.partial(on_device, shape),
        mesh=fine,
        in_specs=(
            P(resp, "kvh"),
            P(resp, "kvh"),
            P(resp, "kvh"),
            P(names, None),
            P(names, None),
            P(resp, "kvh"),
            P(resp, None),
            P(resp, None),
        ),
        out_specs=(
            P(resp, "kvh"),
            P(resp, "kvh"),
            P(resp, "kvh"),
            P(names, None),
            P(names, None),
        ),
        check_vma=False,
    )
```

```python
import functools
import math

import jax
import jax.numpy as jnp
from jax import lax
from jax.experimental import pallas as pl
from jax.experimental.pallas import tpu as pltpu
from jax.sharding import Mesh
from jax.sharding import PartitionSpec as P

QUERY_HEADS = 40
KEY_VALUE_HEADS = 8
HEAD = 128
GROUP = QUERY_HEADS // KEY_VALUE_HEADS
CHUNK = 512
FOLD = 16
PROMPT_TOKENS = 2048
VMEM_MIB = 38
TIE = True
HALF = (GROUP + 1) * HEAD
Q_COLS = slice(0, GROUP * HEAD)
K_COLS = slice(GROUP * HEAD, HALF)
O_COLS = slice(HALF, HALF + GROUP * HEAD)
V_COLS = slice(HALF + GROUP * HEAD, 2 * HALF)
GK_COLS = slice(GROUP * HEAD, (GROUP + 1) * HEAD)
GV_COLS = slice((GROUP + 1) * HEAD, (GROUP + 2) * HEAD)
LOG2E = 1.4426950408889634

NN = (((1,), (0,)), ((), ()))


def dot(a, b, dims):
    return lax.dot_general(a, b, dims, preferred_element_type=jnp.float32)


def attention_kernel(part, *refs):
    if part == 0:
        len_ref, adv_ref, q_hbm, og_hbm, nk_hbm, nv_hbm, kv_hbm = refs[:7]
        gq_hbm, gnk_hbm, gnv_hbm, sum_hbm = refs[7:11]
    else:
        got_ref, got_hbm, kv_hbm, sum_hbm, back_hbm, gkv_hbm = refs[:6]
    (tok_ref, kv_ref, grad_ref, gkv_ref, sum_kv_ref,
     p_ref, d_ref, kt_ref, qt_ref, dot_t_ref, gqt_ref,
     peak_ref, sum_ref, dot_ref, in_sem, kv_sem, out_sem) = refs[-17:]
    tokens = tok_ref.shape[0]
    prompt = kv_ref.shape[0]
    chunks = prompt // CHUNK
    factor = 1.0 / math.sqrt(HEAD)
    scale = factor * LOG2E

    if part == 0:
        mine = lax.axis_index("zl")
        query_cols = pl.ds(pl.multiple_of(mine * (GROUP * HEAD), HEAD), GROUP * HEAD)
        own_cols = pl.ds(pl.multiple_of(mine * HEAD, HEAD), HEAD)
        loads = [
            pltpu.make_async_copy(q_hbm.at[:, query_cols], tok_ref.at[:, Q_COLS], in_sem.at[0]),
            pltpu.make_async_copy(og_hbm.at[:, query_cols], tok_ref.at[:, O_COLS], in_sem.at[1]),
            pltpu.make_async_copy(nk_hbm.at[:, own_cols], tok_ref.at[:, K_COLS], in_sem.at[2]),
            pltpu.make_async_copy(nv_hbm.at[:, own_cols], tok_ref.at[:, V_COLS], in_sem.at[3]),
        ]
    else:
        loads = [pltpu.make_async_copy(got_hbm, tok_ref, in_sem.at[0])]
    for copy in loads:
        copy.start()
    kv_loads, sum_loads = [], []
    for c in range(chunks):
        at = pl.ds(c * CHUNK, CHUNK)
        kv_loads.append(pltpu.make_async_copy(kv_hbm.at[at], kv_ref.at[at], kv_sem.at[c]))
        kv_loads[-1].start()
    if part == 1:
        sum_loads.append(pltpu.make_async_copy(sum_hbm, sum_kv_ref, in_sem.at[1]))
        sum_loads[-1].start()

    def segment(pos, ends):
        seg = jnp.zeros(pos.shape, jnp.int32)
        for end in ends:
            seg = seg + (pos >= end).astype(jnp.int32)
        return seg

    def head_cols(g, first=0):
        return slice(first + g * HEAD, first + (g + 1) * HEAD)

    def tok_cols(g):
        return slice(g * tokens, (g + 1) * tokens)

    def turn(a):
        return a.astype(jnp.float32).T.astype(jnp.bfloat16)

    def forward(keys, values, row, mask):
        size = keys.shape[0]
        groups = size // (8 * FOLD)
        for g in range(GROUP):
            s = dot(keys, qt_ref[:, tok_cols(g)], NN)
            if mask is not None:
                s = jnp.where(mask, s, -1e30)
            d = dot(values, dot_t_ref[:, tok_cols(g)], NN)
            s = s.reshape(groups, FOLD, 8, tokens)
            d_ref[row:row + size, tok_cols(g)] = d
            d = d.reshape(groups, FOLD, 8, tokens)
            for i in range(groups):
                slot = row // FOLD + 8 * i
                key = row + 8 * FOLD * i
                peak = jnp.max(s[i], axis=0)
                e = jnp.exp2((s[i] - peak[None]) * scale)
                p_ref[key:key + 8 * FOLD, tok_cols(g)] = e.reshape(8 * FOLD, tokens)
                peak_ref[slot:slot + 8, tok_cols(g)] = peak
                sum_ref[slot:slot + 8, tok_cols(g)] = jnp.sum(e, axis=0)
                dot_ref[slot:slot + 8, tok_cols(g)] = jnp.sum(e * d[i], axis=0)

    def backward(row, size, deltas):
        groups = size // (8 * FOLD)
        slot = row // FOLD
        key_sum = jnp.zeros((size, HEAD), jnp.float32)
        value_sum = jnp.zeros((size, HEAD), jnp.float32)
        for g in range(GROUP):
            p = p_ref[row:row + size, tok_cols(g)].reshape(groups, FOLD, 8, tokens)
            d = d_ref[row:row + size, tok_cols(g)].reshape(groups, FOLD, 8, tokens)
            share = peak_ref[slot:slot + 8 * groups, tok_cols(g)].reshape(groups, 1, 8, tokens)
            p = p * share
            ds = p * (d - deltas[g][None, None])
            p = p.reshape(size, tokens).astype(jnp.bfloat16)
            ds = ds.reshape(size, tokens).astype(jnp.bfloat16)
            key_sum = key_sum + dot(ds, tok_ref[:, head_cols(g)], NN)
            value_sum = value_sum + dot(p, tok_ref[:, head_cols(g, HALF)], NN)
            query_sum = dot(kt_ref[:, row:row + size], ds, NN)
            if row == kt_ref.shape[1] - tokens:
                gqt_ref[:, tok_cols(g)] = query_sum
            else:
                gqt_ref[:, tok_cols(g)] += query_sum
        return key_sum * factor, value_sum

    stores = []

    def store(source, target):
        stores.append(pltpu.make_async_copy(source, target, out_sem.at[len(stores)]))
        stores[-1].start()

    if part == 0:
        responses = len_ref.shape[1]
        lengths = [len_ref[0, r] for r in range(responses)]
        advantages = [adv_ref[0, r] for r in range(responses)]
    else:
        responses = got_ref.shape[1] // 2
        lengths = [got_ref[0, r].astype(jnp.int32) for r in range(responses)]
        advantages = [got_ref[0, responses + r] for r in range(responses)]
    ends = [sum(lengths[:r + 1]) for r in range(responses)]
    for copy in loads:
        copy.wait()
    tok_seg = segment(lax.broadcasted_iota(jnp.int32, (tokens, HEAD), 0), ends)
    weight = jnp.zeros((tokens, HEAD), jnp.float32)
    for r in range(responses):
        weight = jnp.where(tok_seg == r, advantages[r], weight)
    for g in range(GROUP):
        cols = head_cols(g, HALF)
        do = weight * tok_ref[:, cols].astype(jnp.float32)
        tok_ref[:, cols] = do.astype(jnp.bfloat16)
    for g in range(GROUP):
        qt_ref[:, tok_cols(g)] = turn(tok_ref[:, head_cols(g)])
        dot_t_ref[:, tok_cols(g)] = turn(tok_ref[:, head_cols(g, HALF)])

    u = lax.broadcasted_iota(jnp.int32, (tokens, tokens), 0)
    t = lax.broadcasted_iota(jnp.int32, (tokens, tokens), 1)
    near = (segment(u, ends) == segment(t, ends)) & (u <= t)
    near_keys = tok_ref[:, K_COLS]
    kt_ref[:, prompt:] = turn(near_keys)
    forward(near_keys, tok_ref[:, V_COLS], prompt, near)
    for c in range(chunks):
        at = slice(c * CHUNK, (c + 1) * CHUNK)
        kv_loads[c].wait()
        kt_ref[:, at] = turn(kv_ref[at, :HEAD])
        forward(kv_ref[at, :HEAD], kv_ref[at, HEAD:], c * CHUNK, None)

    deltas = []
    for g in range(GROUP):
        peak = peak_ref[:, tok_cols(g)]
        top = jnp.max(peak, axis=0, keepdims=True)
        share = jnp.exp2((peak - top) * scale)
        row_sum = jnp.sum(share * sum_ref[:, tok_cols(g)], axis=0, keepdims=True)
        weighted = jnp.sum(share * dot_ref[:, tok_cols(g)], axis=0, keepdims=True)
        inverse = 1.0 / row_sum
        peak_ref[:, tok_cols(g)] = share * inverse
        deltas.append(jnp.broadcast_to(weighted * inverse, (8, tokens)))

    for copy in sum_loads:
        copy.wait()
    key_grad, value_grad = backward(prompt, tokens, deltas)
    grad_ref[:, GK_COLS] = key_grad.astype(jnp.bfloat16)
    grad_ref[:, GV_COLS] = value_grad.astype(jnp.bfloat16)
    for c in range(chunks):
        at = slice(c * CHUNK, (c + 1) * CHUNK)
        block = pl.ds(c * CHUNK, CHUNK)
        key_grad, value_grad = backward(c * CHUNK, CHUNK, deltas)
        if part == 0:
            sum_kv_ref[at, :HEAD], sum_kv_ref[at, HEAD:] = key_grad, value_grad
            store(sum_kv_ref.at[block], sum_hbm.at[block])
        else:
            gkv_ref[at, :HEAD] = (sum_kv_ref[at, :HEAD] + key_grad).astype(jnp.bfloat16)
            gkv_ref[at, HEAD:] = (sum_kv_ref[at, HEAD:] + value_grad).astype(jnp.bfloat16)
            store(gkv_ref.at[block], gkv_hbm.at[block])
    for g in range(GROUP):
        grad_ref[:, head_cols(g)] = (gqt_ref[:, tok_cols(g)].T * factor).astype(jnp.bfloat16)
    if part == 0:
        store(grad_ref.at[:, Q_COLS], gq_hbm.at[:, query_cols])
        store(grad_ref.at[:, GK_COLS], gnk_hbm.at[:, own_cols])
        store(grad_ref.at[:, GV_COLS], gnv_hbm.at[:, own_cols])
    else:
        store(grad_ref, back_hbm)
    for copy in stores:
        copy.wait()


def attention(part, smem_args, args, out_shape):
    tokens = args[0].shape[0]
    prompt = PROMPT_TOKENS
    span = prompt + tokens
    wide = GROUP * tokens
    smem = pl.BlockSpec(memory_space=pltpu.SMEM)
    here = pl.BlockSpec(memory_space=pl.ANY)
    bf16, f32 = jnp.bfloat16, jnp.float32
    return pl.pallas_call(
        functools.partial(attention_kernel, part),
        in_specs=[smem] * len(smem_args) + [here] * len(args),
        out_specs=[here] * len(out_shape),
        out_shape=out_shape,
        scratch_shapes=[
            pltpu.VMEM((tokens, 2 * HALF), bf16),
            pltpu.VMEM((prompt, 2 * HEAD), bf16),
            pltpu.VMEM((tokens, (GROUP + 2) * HEAD), bf16),
            pltpu.VMEM((prompt, 2 * HEAD), bf16),
            pltpu.VMEM((prompt, 2 * HEAD), f32),
            pltpu.VMEM((span, wide), f32),
            pltpu.VMEM((span, wide), f32),
            pltpu.VMEM((HEAD, span), bf16),
            pltpu.VMEM((HEAD, wide), bf16),
            pltpu.VMEM((HEAD, wide), bf16),
            pltpu.VMEM((HEAD, wide), f32),
            pltpu.VMEM((span // FOLD, wide), f32),
            pltpu.VMEM((span // FOLD, wide), f32),
            pltpu.VMEM((span // FOLD, wide), f32),
            pltpu.SemaphoreType.DMA((4,)),
            pltpu.SemaphoreType.DMA((prompt // CHUNK,)),
            pltpu.SemaphoreType.DMA((prompt // CHUNK + 3,)),
        ],
        compiler_params=pltpu.CompilerParams(vmem_limit_bytes=VMEM_MIB * 1024 * 1024),
        cost_estimate=pl.CostEstimate(
            flops=2 * 6 * GROUP * tokens * span * HEAD,
            bytes_accessed=4 * 1024 * 1024,
            transcendentals=GROUP * tokens * span,
        ),
        name="attention",
    )(*smem_args, *args)


NEAR = ("zh", "zl", "kvh")
FAR = ("x", "y")
SWAP = [(0, 1), (1, 0)]


def exchange(a, axes):
    return lax.all_to_all(a, axes, split_axis=0, concat_axis=0, tiled=True)


def rows_kernel(copies, key_ref, value_ref, first_ref):
    zl = 2
    kvh = KEY_VALUE_HEADS // zl
    rows = []
    for half in range(zl):
        for owner in range(kvh):
            cols = slice((owner * zl + half) * HEAD, (owner * zl + half + 1) * HEAD)
            rows.append(jnp.concatenate(
                [key_ref[:, cols].astype(jnp.float32), value_ref[:, cols].astype(jnp.float32)], axis=1
            ))
    rows = jnp.concatenate(rows, axis=0)
    count = rows.shape[0]
    rows = rows.astype(jnp.bfloat16)
    for c in range(copies):
        first_ref[c * count:(c + 1) * count, :] = rows


def pack_kernel(len_ref, adv_ref, q_hbm, og_hbm, nk_hbm, nv_hbm, send_ref, scalars_ref, sem):
    other = 1 - lax.axis_index("zl")
    query_cols = pl.ds(pl.multiple_of(other * (GROUP * HEAD), HEAD), GROUP * HEAD)
    key_cols = pl.ds(pl.multiple_of(other * HEAD, HEAD), HEAD)
    moves = [
        pltpu.make_async_copy(q_hbm.at[:, query_cols], send_ref.at[:, Q_COLS], sem.at[0]),
        pltpu.make_async_copy(og_hbm.at[:, query_cols], send_ref.at[:, O_COLS], sem.at[1]),
        pltpu.make_async_copy(nk_hbm.at[:, key_cols], send_ref.at[:, K_COLS], sem.at[2]),
        pltpu.make_async_copy(nv_hbm.at[:, key_cols], send_ref.at[:, V_COLS], sem.at[3]),
    ]
    for move in moves:
        move.start()
    responses = len_ref.shape[1]
    for r in range(responses):
        scalars_ref[0, r] = len_ref[0, r].astype(jnp.float32)
        scalars_ref[0, responses + r] = adv_ref[0, r]
    for move in moves:
        move.wait()


def pack(lengths, advantage, query, out_grad, near_key, near_value):
    smem = pl.BlockSpec(memory_space=pltpu.SMEM)
    vmem = pl.BlockSpec(memory_space=pltpu.VMEM)
    here = pl.BlockSpec(memory_space=pl.ANY)
    return pl.pallas_call(
        pack_kernel,
        in_specs=[smem, smem] + [here] * 4,
        out_specs=[vmem, smem],
        out_shape=[
            jax.ShapeDtypeStruct((query.shape[0], 2 * HALF), jnp.bfloat16),
            jax.ShapeDtypeStruct((1, 2 * lengths.shape[1]), jnp.float32),
        ],
        scratch_shapes=[pltpu.SemaphoreType.DMA((4,))],
        name="pack",
    )(lengths, advantage, query, out_grad, near_key, near_value)


def finish(copies, part):
    rows = jnp.sum(part.astype(jnp.float32).reshape(copies, -1, 2 * HEAD), axis=0)
    zl = 2
    kvh = KEY_VALUE_HEADS // zl
    own = rows.shape[0] // KEY_VALUE_HEADS
    blocks = [
        rows[(half * kvh + owner) * own:(half * kvh + owner + 1) * own]
        for owner in range(kvh) for half in range(zl)
    ]
    return (
        jnp.concatenate([block[:, :HEAD] for block in blocks], axis=1),
        jnp.concatenate([block[:, HEAD:] for block in blocks], axis=1),
    )


def on_device(
    shape, query, response_keys, response_values, prompt_key, prompt_values, out_grad, lengths,
    advantage
):
    x, y, zh, zl, kvh = shape
    own = prompt_key.shape[0]
    first = pl.pallas_call(
        functools.partial(rows_kernel, zh),
        out_shape=jax.ShapeDtypeStruct((zh * KEY_VALUE_HEADS * own, 2 * HEAD), jnp.bfloat16),
        name="rows",
    )(prompt_key, prompt_values)
    block = exchange(first, NEAR)
    send, scalars = pack(lengths, advantage, query, out_grad, response_keys, response_values)
    if TIE:
        block, send, scalars = lax.optimization_barrier((block, send, scalars))
    got = lax.ppermute(send, "zl", SWAP)
    got_scalars = lax.ppermute(scalars, "zl", SWAP)
    kv = exchange(jnp.broadcast_to(block[None], (x * y, *block.shape)).reshape(-1, 2 * HEAD), FAR)

    def like(a, dtype=jnp.bfloat16):
        return jax.ShapeDtypeStruct(a.shape, dtype)

    grad_query, grad_resp_key, grad_resp_value, sums = attention(
        0, (lengths, advantage), (query, out_grad, response_keys, response_values, kv),
        [like(query), like(response_keys), like(response_values), like(kv, jnp.float32)],
    )
    back_shape = jax.ShapeDtypeStruct((query.shape[0], (GROUP + 2) * HEAD), jnp.bfloat16)
    back, grad_kv = attention(1, (got_scalars,), (got, kv, sums), [back_shape, like(kv)])

    back = lax.ppermute(back, "zl", SWAP)
    part = exchange(grad_kv, FAR).reshape(x * y, *block.shape)
    part = jnp.sum(part.astype(jnp.float32), axis=0).astype(jnp.bfloat16)
    grad_prompt_key, grad_prompt_value = finish(zh, exchange(part, NEAR))

    other = 1 - lax.axis_index("zl")
    grad_query = lax.dynamic_update_slice(grad_query, back[:, Q_COLS], (0, other * GROUP * HEAD))
    grad_resp_key = lax.dynamic_update_slice(grad_resp_key, back[:, GK_COLS], (0, other * HEAD))
    grad_resp_value = lax.dynamic_update_slice(grad_resp_value, back[:, GV_COLS], (0, other * HEAD))
    return (grad_query, grad_resp_key, grad_resp_value, grad_prompt_key, grad_prompt_value)


def solution(mesh):
    shape = (4, 2, 4, 2, 4)
    names = ("x", "y", "zh", "zl", "kvh")
    fine = Mesh(mesh.devices.reshape(shape), names)
    resp = names[:4]
    return jax.shard_map(
        functools.partial(on_device, shape),
        mesh=fine,
        in_specs=(
            P(resp, "kvh"),
            P(resp, "kvh"),
            P(resp, "kvh"),
            P(names, None),
            P(names, None),
            P(resp, "kvh"),
            P(resp, None),
            P(resp, None),
        ),
        out_specs=(
            P(resp, "kvh"),
            P(resp, "kvh"),
            P(resp, "kvh"),
            P(names, None),
            P(names, None),
        ),
        check_vma=False,
    )
```

```python
import functools
import math

import jax
import jax.numpy as jnp
from jax import lax
from jax.experimental import pallas as pl
from jax.experimental.pallas import tpu as pltpu
from jax.sharding import Mesh
from jax.sharding import PartitionSpec as P

QUERY_HEADS = 40
KEY_VALUE_HEADS = 8
HEAD = 128
GROUP = QUERY_HEADS // KEY_VALUE_HEADS
CHUNKS = (1024, 2048)
FOLD = 16
PROMPT_TOKENS = 2048
VMEM_MIB = 38
TIE = True
HALF = (GROUP + 1) * HEAD
Q_COLS = slice(0, GROUP * HEAD)
K_COLS = slice(GROUP * HEAD, HALF)
O_COLS = slice(HALF, HALF + GROUP * HEAD)
V_COLS = slice(HALF + GROUP * HEAD, 2 * HALF)
GK_COLS = slice(GROUP * HEAD, (GROUP + 1) * HEAD)
GV_COLS = slice((GROUP + 1) * HEAD, (GROUP + 2) * HEAD)
LOG2E = 1.4426950408889634

NN = (((1,), (0,)), ((), ()))


def dot(a, b, dims):
    return lax.dot_general(a, b, dims, preferred_element_type=jnp.float32)


def attention_kernel(part, *refs):
    if part == 0:
        len_ref, adv_ref, q_hbm, og_hbm, nk_hbm, nv_hbm, kv_hbm = refs[:7]
        gq_hbm, gnk_hbm, gnv_hbm, sum_hbm = refs[7:11]
    else:
        got_ref, got_hbm, kv_hbm, sum_hbm, back_hbm, gkv_hbm = refs[:6]
    (tok_ref, kv_ref, grad_ref, gkv_ref, sum_kv_ref,
     p_ref, d_ref, kt_ref, qt_ref, dot_t_ref, gqt_ref,
     peak_ref, sum_ref, dot_ref, in_sem, kv_sem, out_sem) = refs[-17:]
    tokens = tok_ref.shape[0]
    prompt = kv_ref.shape[0]
    chunk = CHUNKS[part]
    chunks = prompt // chunk
    factor = 1.0 / math.sqrt(HEAD)
    scale = factor * LOG2E

    if part == 0:
        mine = lax.axis_index("zl")
        query_cols = pl.ds(pl.multiple_of(mine * (GROUP * HEAD), HEAD), GROUP * HEAD)
        own_cols = pl.ds(pl.multiple_of(mine * HEAD, HEAD), HEAD)
        loads = [
            pltpu.make_async_copy(q_hbm.at[:, query_cols], tok_ref.at[:, Q_COLS], in_sem.at[0]),
            pltpu.make_async_copy(og_hbm.at[:, query_cols], tok_ref.at[:, O_COLS], in_sem.at[1]),
            pltpu.make_async_copy(nk_hbm.at[:, own_cols], tok_ref.at[:, K_COLS], in_sem.at[2]),
            pltpu.make_async_copy(nv_hbm.at[:, own_cols], tok_ref.at[:, V_COLS], in_sem.at[3]),
        ]
    else:
        loads = [pltpu.make_async_copy(got_hbm, tok_ref, in_sem.at[0])]
    for copy in loads:
        copy.start()
    kv_loads, sum_loads = [], []
    for c in range(chunks):
        at = pl.ds(c * chunk, chunk)
        kv_loads.append(pltpu.make_async_copy(kv_hbm.at[at], kv_ref.at[at], kv_sem.at[c]))
        kv_loads[-1].start()
    if part == 1:
        sum_loads.append(pltpu.make_async_copy(sum_hbm, sum_kv_ref, in_sem.at[1]))
        sum_loads[-1].start()

    def segment(pos, ends):
        seg = jnp.zeros(pos.shape, jnp.int32)
        for end in ends:
            seg = seg + (pos >= end).astype(jnp.int32)
        return seg

    def head_cols(g, first=0):
        return slice(first + g * HEAD, first + (g + 1) * HEAD)

    def tok_cols(g):
        return slice(g * tokens, (g + 1) * tokens)

    def turn(a):
        return a.astype(jnp.float32).T.astype(jnp.bfloat16)

    def forward(keys, values, row, mask):
        size = keys.shape[0]
        groups = size // (8 * FOLD)
        for g in range(GROUP):
            s = dot(keys, qt_ref[:, tok_cols(g)], NN)
            if mask is not None:
                s = jnp.where(mask, s, -1e30)
            d = dot(values, dot_t_ref[:, tok_cols(g)], NN)
            s = s.reshape(groups, FOLD, 8, tokens)
            d_ref[row:row + size, tok_cols(g)] = d
            d = d.reshape(groups, FOLD, 8, tokens)
            for i in range(groups):
                slot = row // FOLD + 8 * i
                key = row + 8 * FOLD * i
                peak = jnp.max(s[i], axis=0)
                e = jnp.exp2((s[i] - peak[None]) * scale)
                p_ref[key:key + 8 * FOLD, tok_cols(g)] = e.reshape(8 * FOLD, tokens)
                peak_ref[slot:slot + 8, tok_cols(g)] = peak
                sum_ref[slot:slot + 8, tok_cols(g)] = jnp.sum(e, axis=0)
                dot_ref[slot:slot + 8, tok_cols(g)] = jnp.sum(e * d[i], axis=0)

    def backward(row, size, deltas):
        groups = size // (8 * FOLD)
        slot = row // FOLD
        key_sum = jnp.zeros((size, HEAD), jnp.float32)
        value_sum = jnp.zeros((size, HEAD), jnp.float32)
        for g in range(GROUP):
            p = p_ref[row:row + size, tok_cols(g)].reshape(groups, FOLD, 8, tokens)
            d = d_ref[row:row + size, tok_cols(g)].reshape(groups, FOLD, 8, tokens)
            share = peak_ref[slot:slot + 8 * groups, tok_cols(g)].reshape(groups, 1, 8, tokens)
            p = p * share
            ds = p * (d - deltas[g][None, None])
            p = p.reshape(size, tokens).astype(jnp.bfloat16)
            ds = ds.reshape(size, tokens).astype(jnp.bfloat16)
            key_sum = key_sum + dot(ds, tok_ref[:, head_cols(g)], NN)
            value_sum = value_sum + dot(p, tok_ref[:, head_cols(g, HALF)], NN)
            query_sum = dot(kt_ref[:, row:row + size], ds, NN)
            if row == kt_ref.shape[1] - tokens:
                gqt_ref[:, tok_cols(g)] = query_sum
            else:
                gqt_ref[:, tok_cols(g)] += query_sum
        return key_sum * factor, value_sum

    stores = []

    def store(source, target):
        stores.append(pltpu.make_async_copy(source, target, out_sem.at[len(stores)]))
        stores[-1].start()

    if part == 0:
        responses = len_ref.shape[1]
        lengths = [len_ref[0, r] for r in range(responses)]
        advantages = [adv_ref[0, r] for r in range(responses)]
    else:
        responses = got_ref.shape[1] // 2
        lengths = [got_ref[0, r].astype(jnp.int32) for r in range(responses)]
        advantages = [got_ref[0, responses + r] for r in range(responses)]
    ends = [sum(lengths[:r + 1]) for r in range(responses)]
    for copy in loads:
        copy.wait()
    tok_seg = segment(lax.broadcasted_iota(jnp.int32, (tokens, HEAD), 0), ends)
    weight = jnp.zeros((tokens, HEAD), jnp.float32)
    for r in range(responses):
        weight = jnp.where(tok_seg == r, advantages[r], weight)
    for g in range(GROUP):
        cols = head_cols(g, HALF)
        do = weight * tok_ref[:, cols].astype(jnp.float32)
        tok_ref[:, cols] = do.astype(jnp.bfloat16)
    for g in range(GROUP):
        qt_ref[:, tok_cols(g)] = turn(tok_ref[:, head_cols(g)])
        dot_t_ref[:, tok_cols(g)] = turn(tok_ref[:, head_cols(g, HALF)])

    u = lax.broadcasted_iota(jnp.int32, (tokens, tokens), 0)
    t = lax.broadcasted_iota(jnp.int32, (tokens, tokens), 1)
    near = (segment(u, ends) == segment(t, ends)) & (u <= t)
    near_keys = tok_ref[:, K_COLS]
    kt_ref[:, prompt:] = turn(near_keys)
    forward(near_keys, tok_ref[:, V_COLS], prompt, near)
    for c in range(chunks):
        at = slice(c * chunk, (c + 1) * chunk)
        kv_loads[c].wait()
        kt_ref[:, at] = turn(kv_ref[at, :HEAD])
        forward(kv_ref[at, :HEAD], kv_ref[at, HEAD:], c * chunk, None)

    deltas = []
    for g in range(GROUP):
        peak = peak_ref[:, tok_cols(g)]
        top = jnp.max(peak, axis=0, keepdims=True)
        share = jnp.exp2((peak - top) * scale)
        row_sum = jnp.sum(share * sum_ref[:, tok_cols(g)], axis=0, keepdims=True)
        weighted = jnp.sum(share * dot_ref[:, tok_cols(g)], axis=0, keepdims=True)
        inverse = 1.0 / row_sum
        peak_ref[:, tok_cols(g)] = share * inverse
        deltas.append(jnp.broadcast_to(weighted * inverse, (8, tokens)))

    for copy in sum_loads:
        copy.wait()
    key_grad, value_grad = backward(prompt, tokens, deltas)
    grad_ref[:, GK_COLS] = key_grad.astype(jnp.bfloat16)
    grad_ref[:, GV_COLS] = value_grad.astype(jnp.bfloat16)
    for c in range(chunks):
        at = slice(c * chunk, (c + 1) * chunk)
        block = pl.ds(c * chunk, chunk)
        key_grad, value_grad = backward(c * chunk, chunk, deltas)
        if part == 0:
            sum_kv_ref[at, :HEAD], sum_kv_ref[at, HEAD:] = key_grad, value_grad
            store(sum_kv_ref.at[block], sum_hbm.at[block])
        else:
            gkv_ref[at, :HEAD] = (sum_kv_ref[at, :HEAD] + key_grad).astype(jnp.bfloat16)
            gkv_ref[at, HEAD:] = (sum_kv_ref[at, HEAD:] + value_grad).astype(jnp.bfloat16)
            store(gkv_ref.at[block], gkv_hbm.at[block])
    for g in range(GROUP):
        grad_ref[:, head_cols(g)] = (gqt_ref[:, tok_cols(g)].T * factor).astype(jnp.bfloat16)
    if part == 0:
        store(grad_ref.at[:, Q_COLS], gq_hbm.at[:, query_cols])
        store(grad_ref.at[:, GK_COLS], gnk_hbm.at[:, own_cols])
        store(grad_ref.at[:, GV_COLS], gnv_hbm.at[:, own_cols])
    else:
        store(grad_ref, back_hbm)
    for copy in stores:
        copy.wait()


def attention(part, smem_args, args, out_shape):
    tokens = args[0].shape[0]
    prompt = PROMPT_TOKENS
    span = prompt + tokens
    wide = GROUP * tokens
    chunks = prompt // CHUNKS[part]
    smem = pl.BlockSpec(memory_space=pltpu.SMEM)
    here = pl.BlockSpec(memory_space=pl.ANY)
    bf16, f32 = jnp.bfloat16, jnp.float32
    return pl.pallas_call(
        functools.partial(attention_kernel, part),
        in_specs=[smem] * len(smem_args) + [here] * len(args),
        out_specs=[here] * len(out_shape),
        out_shape=out_shape,
        scratch_shapes=[
            pltpu.VMEM((tokens, 2 * HALF), bf16),
            pltpu.VMEM((prompt, 2 * HEAD), bf16),
            pltpu.VMEM((tokens, (GROUP + 2) * HEAD), bf16),
            pltpu.VMEM((prompt, 2 * HEAD), bf16),
            pltpu.VMEM((prompt, 2 * HEAD), f32),
            pltpu.VMEM((span, wide), f32),
            pltpu.VMEM((span, wide), f32),
            pltpu.VMEM((HEAD, span), bf16),
            pltpu.VMEM((HEAD, wide), bf16),
            pltpu.VMEM((HEAD, wide), bf16),
            pltpu.VMEM((HEAD, wide), f32),
            pltpu.VMEM((span // FOLD, wide), f32),
            pltpu.VMEM((span // FOLD, wide), f32),
            pltpu.VMEM((span // FOLD, wide), f32),
            pltpu.SemaphoreType.DMA((4,)),
            pltpu.SemaphoreType.DMA((chunks,)),
            pltpu.SemaphoreType.DMA((chunks + 3,)),
        ],
        compiler_params=pltpu.CompilerParams(vmem_limit_bytes=VMEM_MIB * 1024 * 1024),
        cost_estimate=pl.CostEstimate(
            flops=2 * 6 * GROUP * tokens * span * HEAD,
            bytes_accessed=4 * 1024 * 1024,
            transcendentals=GROUP * tokens * span,
        ),
        name="attention",
    )(*smem_args, *args)


NEAR = ("zh", "zl", "kvh")
FAR = ("x", "y")
SWAP = [(0, 1), (1, 0)]


def exchange(a, axes):
    return lax.all_to_all(a, axes, split_axis=0, concat_axis=0, tiled=True)


def rows_kernel(copies, key_ref, value_ref, first_ref):
    zl = 2
    kvh = KEY_VALUE_HEADS // zl
    rows = []
    for half in range(zl):
        for owner in range(kvh):
            cols = slice((owner * zl + half) * HEAD, (owner * zl + half + 1) * HEAD)
            rows.append(jnp.concatenate(
                [key_ref[:, cols].astype(jnp.float32), value_ref[:, cols].astype(jnp.float32)], axis=1
            ))
    rows = jnp.concatenate(rows, axis=0)
    count = rows.shape[0]
    rows = rows.astype(jnp.bfloat16)
    for c in range(copies):
        first_ref[c * count:(c + 1) * count, :] = rows


def pack_kernel(len_ref, adv_ref, q_hbm, og_hbm, nk_hbm, nv_hbm, send_ref, scalars_ref, sem):
    other = 1 - lax.axis_index("zl")
    query_cols = pl.ds(pl.multiple_of(other * (GROUP * HEAD), HEAD), GROUP * HEAD)
    key_cols = pl.ds(pl.multiple_of(other * HEAD, HEAD), HEAD)
    moves = [
        pltpu.make_async_copy(q_hbm.at[:, query_cols], send_ref.at[:, Q_COLS], sem.at[0]),
        pltpu.make_async_copy(og_hbm.at[:, query_cols], send_ref.at[:, O_COLS], sem.at[1]),
        pltpu.make_async_copy(nk_hbm.at[:, key_cols], send_ref.at[:, K_COLS], sem.at[2]),
        pltpu.make_async_copy(nv_hbm.at[:, key_cols], send_ref.at[:, V_COLS], sem.at[3]),
    ]
    for move in moves:
        move.start()
    responses = len_ref.shape[1]
    for r in range(responses):
        scalars_ref[0, r] = len_ref[0, r].astype(jnp.float32)
        scalars_ref[0, responses + r] = adv_ref[0, r]
    for move in moves:
        move.wait()


def pack(lengths, advantage, query, out_grad, near_key, near_value):
    smem = pl.BlockSpec(memory_space=pltpu.SMEM)
    vmem = pl.BlockSpec(memory_space=pltpu.VMEM)
    here = pl.BlockSpec(memory_space=pl.ANY)
    return pl.pallas_call(
        pack_kernel,
        in_specs=[smem, smem] + [here] * 4,
        out_specs=[vmem, smem],
        out_shape=[
            jax.ShapeDtypeStruct((query.shape[0], 2 * HALF), jnp.bfloat16),
            jax.ShapeDtypeStruct((1, 2 * lengths.shape[1]), jnp.float32),
        ],
        scratch_shapes=[pltpu.SemaphoreType.DMA((4,))],
        name="pack",
    )(lengths, advantage, query, out_grad, near_key, near_value)


def finish(copies, part):
    rows = jnp.sum(part.astype(jnp.float32).reshape(copies, -1, 2 * HEAD), axis=0)
    zl = 2
    kvh = KEY_VALUE_HEADS // zl
    own = rows.shape[0] // KEY_VALUE_HEADS
    blocks = [
        rows[(half * kvh + owner) * own:(half * kvh + owner + 1) * own]
        for owner in range(kvh) for half in range(zl)
    ]
    return (
        jnp.concatenate([block[:, :HEAD] for block in blocks], axis=1),
        jnp.concatenate([block[:, HEAD:] for block in blocks], axis=1),
    )


def on_device(
    shape, query, response_keys, response_values, prompt_key, prompt_values, out_grad, lengths,
    advantage
):
    x, y, zh, zl, kvh = shape
    own = prompt_key.shape[0]
    first = pl.pallas_call(
        functools.partial(rows_kernel, zh),
        out_shape=jax.ShapeDtypeStruct((zh * KEY_VALUE_HEADS * own, 2 * HEAD), jnp.bfloat16),
        name="rows",
    )(prompt_key, prompt_values)
    block = exchange(first, NEAR)
    send, scalars = pack(lengths, advantage, query, out_grad, response_keys, response_values)
    if TIE:
        block, send, scalars = lax.optimization_barrier((block, send, scalars))
    got = lax.ppermute(send, "zl", SWAP)
    got_scalars = lax.ppermute(scalars, "zl", SWAP)
    kv = exchange(jnp.broadcast_to(block[None], (x * y, *block.shape)).reshape(-1, 2 * HEAD), FAR)

    def like(a, dtype=jnp.bfloat16):
        return jax.ShapeDtypeStruct(a.shape, dtype)

    grad_query, grad_resp_key, grad_resp_value, sums = attention(
        0, (lengths, advantage), (query, out_grad, response_keys, response_values, kv),
        [like(query), like(response_keys), like(response_values), like(kv, jnp.float32)],
    )
    back_shape = jax.ShapeDtypeStruct((query.shape[0], (GROUP + 2) * HEAD), jnp.bfloat16)
    back, grad_kv = attention(1, (got_scalars,), (got, kv, sums), [back_shape, like(kv)])

    back = lax.ppermute(back, "zl", SWAP)
    part = exchange(grad_kv, FAR).reshape(x * y, *block.shape)
    part = jnp.sum(part.astype(jnp.float32), axis=0).astype(jnp.bfloat16)
    grad_prompt_key, grad_prompt_value = finish(zh, exchange(part, NEAR))

    other = 1 - lax.axis_index("zl")
    grad_query = lax.dynamic_update_slice(grad_query, back[:, Q_COLS], (0, other * GROUP * HEAD))
    grad_resp_key = lax.dynamic_update_slice(grad_resp_key, back[:, GK_COLS], (0, other * HEAD))
    grad_resp_value = lax.dynamic_update_slice(grad_resp_value, back[:, GV_COLS], (0, other * HEAD))
    return (grad_query, grad_resp_key, grad_resp_value, grad_prompt_key, grad_prompt_value)


def solution(mesh):
    shape = (4, 2, 4, 2, 4)
    names = ("x", "y", "zh", "zl", "kvh")
    fine = Mesh(mesh.devices.reshape(shape), names)
    resp = names[:4]
    return jax.shard_map(
        functools.partial(on_device, shape),
        mesh=fine,
        in_specs=(
            P(resp, "kvh"),
            P(resp, "kvh"),
            P(resp, "kvh"),
            P(names, None),
            P(names, None),
            P(resp, "kvh"),
            P(resp, None),
            P(resp, None),
        ),
        out_specs=(
            P(resp, "kvh"),
            P(resp, "kvh"),
            P(resp, "kvh"),
            P(names, None),
            P(names, None),
        ),
        check_vma=False,
    )
```

```python
import functools
import math

import jax
import jax.numpy as jnp
from jax import lax
from jax.experimental import pallas as pl
from jax.experimental.pallas import tpu as pltpu
from jax.sharding import Mesh
from jax.sharding import PartitionSpec as P

QUERY_HEADS = 40
KEY_VALUE_HEADS = 8
HEAD = 128
GROUP = QUERY_HEADS // KEY_VALUE_HEADS
CHUNKS = (1024, 2048)
FOLD = 16
PROMPT_TOKENS = 2048
VMEM_MIB = 38
HALF = (GROUP + 1) * HEAD
Q_COLS = slice(0, GROUP * HEAD)
K_COLS = slice(GROUP * HEAD, HALF)
O_COLS = slice(HALF, HALF + GROUP * HEAD)
V_COLS = slice(HALF + GROUP * HEAD, 2 * HALF)
GK_COLS = slice(GROUP * HEAD, (GROUP + 1) * HEAD)
GV_COLS = slice((GROUP + 1) * HEAD, (GROUP + 2) * HEAD)
LOG2E = 1.4426950408889634

NN = (((1,), (0,)), ((), ()))


def dot(a, b, dims):
    return lax.dot_general(a, b, dims, preferred_element_type=jnp.float32)


def attention_kernel(part, prompt_side, token_side, *refs):
    refs = list(refs)
    take = functools.partial(refs.pop, 0)
    len_ref, tok_hbm, kv_hbm = take(), take(), take()
    if part == 1:
        sum_hbm, back_hbm, gkv_hbm = take(), take(), take()
    elif token_side:
        gq_hbm, gnk_hbm, gnv_hbm = take(), take(), take()
    else:
        sum_hbm = take()
    (tok_ref, kv_ref, grad_ref, gkv_ref, sum_kv_ref,
     p_ref, d_ref, kt_ref, qt_ref, dot_t_ref, gqt_ref,
     peak_ref, sum_ref, dot_ref, in_sem, kv_sem, out_sem) = refs
    tokens = tok_ref.shape[0]
    prompt = kv_ref.shape[0]
    chunk = CHUNKS[part]
    chunks = prompt // chunk
    factor = 1.0 / math.sqrt(HEAD)
    scale = factor * LOG2E

    if part == 0:
        mine = lax.axis_index("zl")
        query_cols = pl.ds(pl.multiple_of(mine * (GROUP * HEAD), HEAD), GROUP * HEAD)
        own_cols = pl.ds(pl.multiple_of(mine * HEAD, HEAD), HEAD)
    loads = [pltpu.make_async_copy(tok_hbm, tok_ref, in_sem.at[0])]
    for copy in loads:
        copy.start()
    kv_loads, sum_loads = [], []
    for c in range(chunks):
        at = pl.ds(c * chunk, chunk)
        kv_loads.append(pltpu.make_async_copy(kv_hbm.at[at], kv_ref.at[at], kv_sem.at[c]))
        kv_loads[-1].start()
    if part == 1:
        sum_loads.append(pltpu.make_async_copy(sum_hbm, sum_kv_ref, in_sem.at[1]))
        sum_loads[-1].start()

    def segment(pos, ends):
        seg = jnp.zeros(pos.shape, jnp.int32)
        for end in ends:
            seg = seg + (pos >= end).astype(jnp.int32)
        return seg

    def head_cols(g, first=0):
        return slice(first + g * HEAD, first + (g + 1) * HEAD)

    def tok_cols(g):
        return slice(g * tokens, (g + 1) * tokens)

    def turn(a):
        return a.astype(jnp.float32).T.astype(jnp.bfloat16)

    def forward(keys, values, row, mask):
        size = keys.shape[0]
        groups = size // (8 * FOLD)
        for g in range(GROUP):
            s = dot(keys, qt_ref[:, tok_cols(g)], NN)
            if mask is not None:
                s = jnp.where(mask, s, -1e30)
            d = dot(values, dot_t_ref[:, tok_cols(g)], NN)
            s = s.reshape(groups, FOLD, 8, tokens)
            d_ref[row:row + size, tok_cols(g)] = d
            d = d.reshape(groups, FOLD, 8, tokens)
            for i in range(groups):
                slot = row // FOLD + 8 * i
                key = row + 8 * FOLD * i
                peak = jnp.max(s[i], axis=0)
                e = jnp.exp2((s[i] - peak[None]) * scale)
                p_ref[key:key + 8 * FOLD, tok_cols(g)] = e.reshape(8 * FOLD, tokens)
                peak_ref[slot:slot + 8, tok_cols(g)] = peak
                sum_ref[slot:slot + 8, tok_cols(g)] = jnp.sum(e, axis=0)
                dot_ref[slot:slot + 8, tok_cols(g)] = jnp.sum(e * d[i], axis=0)

    def backward(row, size, deltas):
        groups = size // (8 * FOLD)
        slot = row // FOLD
        near = row == prompt
        key_sum = jnp.zeros((size, HEAD), jnp.float32)
        value_sum = jnp.zeros((size, HEAD), jnp.float32)
        for g in range(GROUP):
            p = p_ref[row:row + size, tok_cols(g)].reshape(groups, FOLD, 8, tokens)
            d = d_ref[row:row + size, tok_cols(g)].reshape(groups, FOLD, 8, tokens)
            share = peak_ref[slot:slot + 8 * groups, tok_cols(g)].reshape(groups, 1, 8, tokens)
            p = p * share
            ds = p * (d - deltas[g][None, None])
            ds = ds.reshape(size, tokens).astype(jnp.bfloat16)
            if near or prompt_side:
                p = p.reshape(size, tokens).astype(jnp.bfloat16)
                key_sum = key_sum + dot(ds, tok_ref[:, head_cols(g)], NN)
                value_sum = value_sum + dot(p, tok_ref[:, head_cols(g, HALF)], NN)
            if token_side:
                query_sum = dot(kt_ref[:, row:row + size], ds, NN)
                if near:
                    gqt_ref[:, tok_cols(g)] = query_sum
                else:
                    gqt_ref[:, tok_cols(g)] += query_sum
        return key_sum * factor, value_sum

    stores = []

    def store(source, target):
        stores.append(pltpu.make_async_copy(source, target, out_sem.at[len(stores)]))
        stores[-1].start()

    responses = len_ref.shape[1]
    lengths = [len_ref[0, r] for r in range(responses)]
    ends = [sum(lengths[:r + 1]) for r in range(responses)]
    for copy in loads:
        copy.wait()
    for g in range(GROUP):
        qt_ref[:, tok_cols(g)] = turn(tok_ref[:, head_cols(g)])
        dot_t_ref[:, tok_cols(g)] = turn(tok_ref[:, head_cols(g, HALF)])

    u = lax.broadcasted_iota(jnp.int32, (tokens, tokens), 0)
    t = lax.broadcasted_iota(jnp.int32, (tokens, tokens), 1)
    near = (segment(u, ends) == segment(t, ends)) & (u <= t)
    near_keys = tok_ref[:, K_COLS]
    kt_ref[:, prompt:] = turn(near_keys)
    forward(near_keys, tok_ref[:, V_COLS], prompt, near)
    for c in range(chunks):
        at = slice(c * chunk, (c + 1) * chunk)
        kv_loads[c].wait()
        if token_side:
            kt_ref[:, at] = turn(kv_ref[at, :HEAD])
        forward(kv_ref[at, :HEAD], kv_ref[at, HEAD:], c * chunk, None)

    deltas = []
    for g in range(GROUP):
        peak = peak_ref[:, tok_cols(g)]
        top = jnp.max(peak, axis=0, keepdims=True)
        share = jnp.exp2((peak - top) * scale)
        row_sum = jnp.sum(share * sum_ref[:, tok_cols(g)], axis=0, keepdims=True)
        weighted = jnp.sum(share * dot_ref[:, tok_cols(g)], axis=0, keepdims=True)
        inverse = 1.0 / row_sum
        peak_ref[:, tok_cols(g)] = share * inverse
        deltas.append(jnp.broadcast_to(weighted * inverse, (8, tokens)))

    for copy in sum_loads:
        copy.wait()
    if token_side:
        key_grad, value_grad = backward(prompt, tokens, deltas)
        grad_ref[:, GK_COLS] = key_grad.astype(jnp.bfloat16)
        grad_ref[:, GV_COLS] = value_grad.astype(jnp.bfloat16)
    for c in range(chunks):
        at = slice(c * chunk, (c + 1) * chunk)
        block = pl.ds(c * chunk, chunk)
        key_grad, value_grad = backward(c * chunk, chunk, deltas)
        if not prompt_side:
            continue
        if part == 0:
            sum_kv_ref[at, :HEAD], sum_kv_ref[at, HEAD:] = key_grad, value_grad
            store(sum_kv_ref.at[block], sum_hbm.at[block])
        else:
            gkv_ref[at, :HEAD] = (sum_kv_ref[at, :HEAD] + key_grad).astype(jnp.bfloat16)
            gkv_ref[at, HEAD:] = (sum_kv_ref[at, HEAD:] + value_grad).astype(jnp.bfloat16)
            store(gkv_ref.at[block], gkv_hbm.at[block])
    if token_side:
        for g in range(GROUP):
            grad_ref[:, head_cols(g)] = (gqt_ref[:, tok_cols(g)].T * factor).astype(jnp.bfloat16)
        if part == 0:
            store(grad_ref.at[:, Q_COLS], gq_hbm.at[:, query_cols])
            store(grad_ref.at[:, GK_COLS], gnk_hbm.at[:, own_cols])
            store(grad_ref.at[:, GV_COLS], gnv_hbm.at[:, own_cols])
        else:
            store(grad_ref, back_hbm)
    for copy in stores:
        copy.wait()


def attention(part, prompt_side, token_side, smem_args, args, out_shape):
    tokens = args[0].shape[0]
    prompt = PROMPT_TOKENS
    span = prompt + tokens
    wide = GROUP * tokens
    chunks = prompt // CHUNKS[part]
    smem = pl.BlockSpec(memory_space=pltpu.SMEM)
    here = pl.BlockSpec(memory_space=pl.ANY)
    bf16, f32 = jnp.bfloat16, jnp.float32
    return pl.pallas_call(
        functools.partial(attention_kernel, part, prompt_side, token_side),
        in_specs=[smem] * len(smem_args) + [here] * len(args),
        out_specs=[here] * len(out_shape),
        out_shape=out_shape,
        scratch_shapes=[
            pltpu.VMEM((tokens, 2 * HALF), bf16),
            pltpu.VMEM((prompt, 2 * HEAD), bf16),
            pltpu.VMEM((tokens, (GROUP + 2) * HEAD), bf16),
            pltpu.VMEM((prompt, 2 * HEAD), bf16),
            pltpu.VMEM((prompt, 2 * HEAD), f32),
            pltpu.VMEM((span, wide), f32),
            pltpu.VMEM((span, wide), f32),
            pltpu.VMEM((HEAD, span), bf16),
            pltpu.VMEM((HEAD, wide), bf16),
            pltpu.VMEM((HEAD, wide), bf16),
            pltpu.VMEM((HEAD, wide), f32),
            pltpu.VMEM((span // FOLD, wide), f32),
            pltpu.VMEM((span // FOLD, wide), f32),
            pltpu.VMEM((span // FOLD, wide), f32),
            pltpu.SemaphoreType.DMA((4,)),
            pltpu.SemaphoreType.DMA((chunks,)),
            pltpu.SemaphoreType.DMA((chunks + 3,)),
        ],
        compiler_params=pltpu.CompilerParams(vmem_limit_bytes=VMEM_MIB * 1024 * 1024),
        cost_estimate=pl.CostEstimate(
            flops=2 * 6 * GROUP * tokens * span * HEAD,
            bytes_accessed=4 * 1024 * 1024,
            transcendentals=GROUP * tokens * span,
        ),
        name="attention",
    )(*smem_args, *args)


NEAR = ("zh", "zl", "kvh")
FAR = ("x", "y")
SWAP = [(0, 1), (1, 0)]


def exchange(a, axes):
    return lax.all_to_all(a, axes, split_axis=0, concat_axis=0, tiled=True)


def rows_kernel(copies, key_ref, value_ref, first_ref):
    zl = 2
    kvh = KEY_VALUE_HEADS // zl
    rows = []
    for half in range(zl):
        for owner in range(kvh):
            cols = slice((owner * zl + half) * HEAD, (owner * zl + half + 1) * HEAD)
            rows.append(jnp.concatenate(
                [key_ref[:, cols].astype(jnp.float32), value_ref[:, cols].astype(jnp.float32)], axis=1
            ))
    rows = jnp.concatenate(rows, axis=0)
    count = rows.shape[0]
    rows = rows.astype(jnp.bfloat16)
    for c in range(copies):
        first_ref[c * count:(c + 1) * count, :] = rows


def pack_kernel(
    len_ref, adv_ref, q_hbm, og_hbm, nk_hbm, nv_hbm, own_ref, send_ref, sem
):
    mine = lax.axis_index("zl")
    loads, late = [], []
    for i, (head, held) in enumerate([(1 - mine, send_ref), (mine, own_ref)]):
        query_cols = pl.ds(pl.multiple_of(head * (GROUP * HEAD), HEAD), GROUP * HEAD)
        key_cols = pl.ds(pl.multiple_of(head * HEAD, HEAD), HEAD)
        loads.append(pltpu.make_async_copy(og_hbm.at[:, query_cols], held.at[:, O_COLS], sem.at[i]))
        for j, (source, cols, at) in enumerate(
            [(q_hbm, query_cols, Q_COLS), (nk_hbm, key_cols, K_COLS), (nv_hbm, key_cols, V_COLS)]
        ):
            late.append(
                pltpu.make_async_copy(source.at[:, cols], held.at[:, at], sem.at[2 + 3 * i + j])
            )
    for copy in loads + late:
        copy.start()
    shape = (own_ref.shape[0], HEAD)
    tok = lax.broadcasted_iota(jnp.int32, shape, 0)
    weight = jnp.zeros(shape, jnp.float32)
    end = 0
    for r in range(len_ref.shape[1]):
        begin, end = end, end + len_ref[0, r]
        weight = jnp.where((tok >= begin) & (tok < end), adv_ref[0, r], weight)
    for copy, held in zip(loads, (send_ref, own_ref)):
        copy.wait()
        for g in range(GROUP):
            cols = slice(HALF + g * HEAD, HALF + (g + 1) * HEAD)
            held[:, cols] = (weight * held[:, cols].astype(jnp.float32)).astype(jnp.bfloat16)
    for copy in late:
        copy.wait()


def pack(lengths, advantage, query, out_grad, near_key, near_value):
    smem = pl.BlockSpec(memory_space=pltpu.SMEM)
    vmem = pl.BlockSpec(memory_space=pltpu.VMEM)
    here = pl.BlockSpec(memory_space=pl.ANY)
    shape = jax.ShapeDtypeStruct((query.shape[0], 2 * HALF), jnp.bfloat16)
    return pl.pallas_call(
        pack_kernel,
        in_specs=[smem, smem] + [here] * 4,
        out_specs=[vmem, vmem],
        out_shape=[shape, shape],
        scratch_shapes=[pltpu.SemaphoreType.DMA((8,))],
        name="pack",
    )(lengths, advantage, query, out_grad, near_key, near_value)


def finish(copies, part):
    rows = jnp.sum(part.astype(jnp.float32).reshape(copies, -1, 2 * HEAD), axis=0)
    zl = 2
    kvh = KEY_VALUE_HEADS // zl
    own = rows.shape[0] // KEY_VALUE_HEADS
    blocks = [
        rows[(half * kvh + owner) * own:(half * kvh + owner + 1) * own]
        for owner in range(kvh) for half in range(zl)
    ]
    return (
        jnp.concatenate([block[:, :HEAD] for block in blocks], axis=1),
        jnp.concatenate([block[:, HEAD:] for block in blocks], axis=1),
    )


def on_device(
    shape, query, response_keys, response_values, prompt_key, prompt_values, out_grad, lengths,
    advantage
):
    x, y, zh, zl, kvh = shape
    own = prompt_key.shape[0]
    first = pl.pallas_call(
        functools.partial(rows_kernel, zh),
        out_shape=jax.ShapeDtypeStruct((zh * KEY_VALUE_HEADS * own, 2 * HEAD), jnp.bfloat16),
        name="rows",
    )(prompt_key, prompt_values)
    block = exchange(first, NEAR)
    kept, send = pack(lengths, advantage, query, out_grad, response_keys, response_values)
    block, kept, send, late_lengths = lax.optimization_barrier((block, kept, send, lengths))
    got = lax.ppermute(send, "zl", SWAP)
    got_lengths = lax.ppermute(late_lengths, "zl", SWAP)
    kv = exchange(jnp.broadcast_to(block[None], (x * y, *block.shape)).reshape(-1, 2 * HEAD), FAR)

    def like(a, dtype=jnp.bfloat16):
        return jax.ShapeDtypeStruct(a.shape, dtype)

    sums, = attention(0, True, False, (lengths,), (kept, kv), [like(kv, jnp.float32)])
    back_shape = jax.ShapeDtypeStruct((query.shape[0], (GROUP + 2) * HEAD), jnp.bfloat16)
    back, grad_kv = attention(
        1, True, True, (got_lengths,), (got, kv, sums), [back_shape, like(kv)]
    )
    kv, grad_kv = lax.optimization_barrier((kv, grad_kv))
    grad_query, grad_resp_key, grad_resp_value = attention(
        0, False, True, (lengths,), (kept, kv),
        [like(query), like(response_keys), like(response_values)],
    )
    back = lax.ppermute(back, "zl", SWAP)
    part = exchange(grad_kv, FAR).reshape(x * y, *block.shape)
    part = jnp.sum(part.astype(jnp.float32), axis=0).astype(jnp.bfloat16)
    grad_prompt_key, grad_prompt_value = finish(zh, exchange(part, NEAR))

    other = 1 - lax.axis_index("zl")
    grad_query = lax.dynamic_update_slice(grad_query, back[:, Q_COLS], (0, other * GROUP * HEAD))
    grad_resp_key = lax.dynamic_update_slice(grad_resp_key, back[:, GK_COLS], (0, other * HEAD))
    grad_resp_value = lax.dynamic_update_slice(grad_resp_value, back[:, GV_COLS], (0, other * HEAD))
    return (grad_query, grad_resp_key, grad_resp_value, grad_prompt_key, grad_prompt_value)


def solution(mesh):
    shape = (4, 2, 4, 2, 4)
    names = ("x", "y", "zh", "zl", "kvh")
    fine = Mesh(mesh.devices.reshape(shape), names)
    resp = names[:4]
    return jax.shard_map(
        functools.partial(on_device, shape),
        mesh=fine,
        in_specs=(
            P(resp, "kvh"),
            P(resp, "kvh"),
            P(resp, "kvh"),
            P(names, None),
            P(names, None),
            P(resp, "kvh"),
            P(resp, None),
            P(resp, None),
        ),
        out_specs=(
            P(resp, "kvh"),
            P(resp, "kvh"),
            P(resp, "kvh"),
            P(names, None),
            P(names, None),
        ),
        check_vma=False,
    )
```
